128 devices in a mesh: dp: 8 (over z, x_hi), expert: 16 (over y, x_lo, core).
Axes of the slice: x: 4 (x_hi: 2, x_lo: 2; x = x_hi * 2 + x_lo), y: 4, z: 4, core: 2. Of those that a mesh axis runs over, the one named last changes fastest.
Arguments:
- tokens: bfloat16 [16384, 2560], P(('dp', 'expert')), may hold values from -6 to 6
- expert_ids: int32 [16384, 6], P(('dp', 'expert')), may hold values from 0 to 15, all different within a row; in each aligned block of 128 rows (0 to 127, 128 to 255, ...) at most 56 rows name the same one
- gate_q: int32 [16384, 6], P(('dp', 'expert')), may hold values from 8192 to 65535
- cotangent: bfloat16 [16384, 2560], P(('dp', 'expert')), may hold values from -6 to 6
- placement: int32 [16], replicated, may hold values from 0 to 15, as said below
- weights: bfloat16 [16, 2560, 2304], P('expert'), may hold values from -4 to 4
- moment_one: float32 [16, 2560, 2304], P('expert', 'dp'), may hold values from -1 to 1
- moment_two: float32 [16, 2560, 2304], P('expert', 'dp'), may hold values from 0.001 to 0.3
Outputs:
- token_grad: bfloat16 [16384, 2560], P(('dp', 'expert'))
- new_weights: bfloat16 [16, 2560, 2304], P('expert', 'dp')
- new_moment_one: float32 [16, 2560, 2304], P('expert', 'dp')
- new_moment_two: float32 [16, 2560, 2304], P('expert', 'dp')
The draws below stay inside these ranges and needn't reach their ends.
Inputs may be any that keep to these rules, and one draw needn't show every extreme that they name: `expert_ids`: in each aligned block of 128 rows (the tokens of one device) no expert is named by more than 56 (token, choice) pairs; some expert is named by exactly 56 in some blocks. placement[e] is e or (e + 8) modulo 16; if e goes to f then f goes to e; in every draw some experts move and some stay.
All inputs are finite; a program needn't handle non-finite values.
Results may differ from the reference program's by a relative error of at most 0.024.
Values may be sent and summed in bfloat16 or wider, within the bound.
A program may use at most 192 MiB of HBM per device.

```python
import math
import jax
import jax.numpy as jnp
import numpy as np
from jax import lax

D = 2560
HW = 768
TOP = 6
TOK_DEV = 128
EXPERTS = 16
CAP = 56
TOKENS = 16384
N_DP = 8
N_EXPERT = 16


def draw_placement(key, part):
    key = jax.random.fold_in(key, 11)
    half_count = EXPERTS // 2
    moving = jax.random.randint(key, (half_count,), 0, 2).astype(jnp.int32)
    moving = moving.at[0].set(1).at[1].set(0)
    slots = jnp.arange(EXPERTS, dtype=jnp.int32)
    flags = moving[slots % half_count]
    return jnp.where(flags == 1, (slots + half_count) % EXPERTS, slots).astype(jnp.int32)


def set_ends(values, stream_key, smallest, largest):
    index_at = [jax.random.randint(jax.random.fold_in(stream_key, axis), (), 0, length) for axis, length in enumerate(values.shape)]
    widest = values.shape.index(max(values.shape))
    neighbour = index_at[:widest] + [(index_at[widest] + 1) % values.shape[widest]] + index_at[widest + 1:]
    return values.at[tuple(index_at)].set(smallest).at[tuple(neighbour)].set(largest)


def steps_of(stream_key, extent, pieces, least, largest):
    level = 1.0
    for dim, blocks in pieces:
        heights = jax.random.uniform(jax.random.fold_in(jax.random.fold_in(stream_key, 6), dim), (blocks,), jnp.float32, least / len(pieces), largest / len(pieces))
        level = level * jnp.repeat(jnp.exp(heights), extent[dim] // blocks).reshape((-1,) + (1,) * (len(extent) - 1 - dim))
    return level


def assign_block(stream_key, own, number, rows, amount, top, reach, slope):
    sequence = jax.random.permutation(stream_key, amount)
    crowded, common = load_shares(amount, rows * top, reach, slope, True), load_shares(amount, rows * top, reach, slope, False)
    places = jnp.arange(amount)

    def named(sizes, rotation):
        used = int((sizes > 0).sum())
        fixed = max(1, used // 4)
        shifted = fixed + (places - fixed + rotation * (used - fixed)) % max(1, amount - fixed)
        return jnp.zeros((amount,), jnp.int32).at[sequence[jnp.where(places < fixed, places, shifted)]].set(jnp.asarray(sizes, jnp.int32))

    sizes = jnp.where(number % 4 == 0, named(crowded, number // 4), named(common, number - number // 4 - 1))
    mixed = jax.random.permutation(jax.random.fold_in(own, 3), amount)
    source_of, receiver = mixed[0:amount // 2 * 2:2], mixed[1:amount // 2 * 2:2]
    room = jnp.minimum(sizes[source_of] - 1, reach - sizes[receiver]) // 2
    room = jnp.where((source_of == sequence[0]) | (receiver == sequence[0]) | (sizes[receiver] == 0), 0, jnp.maximum(room, 0))
    shifted = jax.random.randint(jax.random.fold_in(own, 4), (amount // 2,), 0, 1 << 20) % (room + 1)
    sizes = sizes.at[source_of].add(-shifted).at[receiver].add(shifted)
    labels = jnp.searchsorted(jnp.cumsum(sizes), jnp.arange(rows * top), side="right").astype(jnp.int32)
    listing = labels.reshape(top, rows).T
    listing = listing[jax.random.permutation(jax.random.fold_in(own, 1), rows)]
    rotation = jax.random.randint(jax.random.fold_in(own, 2), (rows, 1), 0, top)
    return jnp.take_along_axis(listing, (jnp.arange(top)[None, :] + rotation) % top, axis=1)


def load_shares(number_of, total, bound, slope, full):
    weights = [(1 << 20) // math.isqrt(rank ** slope) + 1 for rank in range(1, number_of + 1)]
    largest = bound if full else min(bound, max(-(-total // number_of), total * weights[0] // sum(weights)))
    least = 1 if total - largest >= number_of - 1 else 0
    holding, rest = [largest] + [least] * (number_of - 1), total - largest - least * (number_of - 1)
    while rest > 0:
        movable = [i for i in range(1, number_of) if holding[i] < largest] or [i for i in range(1, number_of) if holding[i] < bound]
        pool, left = sum([weights[i] for i in movable]), rest
        for i in movable:
            addition = min(bound - holding[i], max(1, left * weights[i] // pool), rest)
            holding[i] = holding[i] + addition
            rest = rest - addition
    return np.array(holding)


def gaussian(stream_key, extent, width, reach, cuts=(), held_as=jnp.bfloat16):
    drawn = width * jax.random.normal(stream_key, extent, jnp.float32)
    if cuts:
        drawn = drawn * steps_of(stream_key, extent, cuts, -0.22, 0.18)
    return jnp.clip(drawn, -reach, reach).astype(held_as)


def setup_inputs(seed: int = 0) -> dict:
    key_of = jax.random.split(jax.random.key(seed), 9)
    tokens = gaussian(key_of[0], (TOKENS, D), 1.0, 6.0, ((0, 128),))
    expert_ids_keys = jax.random.split(jax.random.fold_in(key_of[1], 1), TOKENS // TOK_DEV)
    expert_ids_turns = jax.random.permutation(jax.random.fold_in(key_of[1], 3), TOKENS // TOK_DEV)
    expert_ids = jax.vmap(lambda own, number: assign_block(jax.random.fold_in(key_of[1], 2), own, number, TOK_DEV, N_EXPERT, TOP, CAP, 2))(expert_ids_keys, expert_ids_turns).reshape((TOKENS, TOP))
    gate_q = set_ends(jax.random.randint(key_of[2], (TOKENS, TOP), 8192, 65536), jax.random.fold_in(key_of[2], 1), 8192, 65535).astype(jnp.int32)
    cotangent = gaussian(key_of[3], (TOKENS, D), 1.0, 6.0, ((0, 128),))
    placement = draw_placement(jax.random.fold_in(key_of[8], 71), 0)
    weights = gaussian(key_of[5], (EXPERTS, D, 3 * HW), 1.0, 4.0, ((0, 16),))
    moment_one = gaussian(key_of[6], (EXPERTS, D, 3 * HW), 0.2, 1.0, ((0, 16), (1, 8)), jnp.float32)
    moment_two = jnp.clip(jnp.exp(math.log(0.3) - 5.7037825 * jax.random.uniform(key_of[7], (EXPERTS, D, 3 * HW), jnp.float32) ** steps_of(key_of[7], (EXPERTS, D, 3 * HW), ((0, 16), (1, 8)), -0.2, 0.2)), 0.001, 0.3)
    return dict(tokens=tokens, expert_ids=expert_ids, gate_q=gate_q, cotangent=cotangent, placement=placement, weights=weights, moment_one=moment_one, moment_two=moment_two)


beta_one = 0.9
beta_two = 0.95
learn_rate = 0.02
decay_rate = 0.1
adam_eps = 1e-08
adam_step = 20.0

def slot_index(choices, expert_count, capacity):
    flat_ids = choices.reshape(-1).astype(jnp.int32)
    onehot = (flat_ids[:, None] == jnp.arange(expert_count, dtype=jnp.int32)[None, :]).astype(jnp.int32)
    earlier = jnp.cumsum(onehot, axis=0) - onehot
    position = lax.optimization_barrier(jnp.sum(earlier * onehot, axis=1))
    return (flat_ids * capacity + position).astype(jnp.int32)

def fill_slots(rows_in, cot_rows, gate_ints, slots, slot_count, top_k):
    pairs = slots.shape[0]
    owner = jnp.zeros((slot_count,), jnp.int32).at[slots].set(jnp.arange(pairs, dtype=jnp.int32) // top_k + 1)
    live = owner > 0
    source = jnp.maximum(owner - 1, 0)
    gates = jnp.zeros((slot_count,), jnp.float32).at[slots].set(gate_ints.reshape(-1).astype(jnp.float32) / 65536.0)
    inputs = jnp.where(live[:, None], rows_in[source], jnp.zeros((), rows_in.dtype))
    scaled = (gates[:, None] * cot_rows[source].astype(jnp.float32)).astype(jnp.bfloat16)
    return (inputs, scaled)

def expert_pass(inputs, cots, expert_weights):
    model_width = expert_weights.shape[0]
    hidden_units = expert_weights.shape[1] // 3
    scale_width = model_width ** (-0.5)
    scale_hidden = hidden_units ** (-0.5)
    weight_f = expert_weights.astype(jnp.float32)
    input_f = inputs.astype(jnp.float32)
    cot_f = cots.astype(jnp.float32)
    in_cols = weight_f[:, :2 * hidden_units]
    down_cols = weight_f[:, 2 * hidden_units:]
    pre = jnp.dot(input_f, in_cols) * scale_width
    gate_part = pre[:, :hidden_units]
    up_part = pre[:, hidden_units:]
    sig = jax.nn.sigmoid(gate_part)
    act = (gate_part * sig * up_part).astype(jnp.bfloat16)
    d_act = jnp.dot(cot_f, down_cols) * scale_hidden
    d_gate = d_act * up_part * sig * (1.0 + gate_part * (1.0 - sig))
    d_up = d_act * gate_part * sig
    d_hidden = jnp.concatenate([d_gate, d_up], axis=1).astype(jnp.bfloat16)
    d_hidden_f = d_hidden.astype(jnp.float32)
    partial_dx = (jnp.dot(d_hidden_f, in_cols.T) * scale_width).astype(jnp.bfloat16)
    grad_in = jnp.dot(input_f.T, d_hidden_f) * scale_width
    grad_down = jnp.dot(cot_f.T, act.astype(jnp.float32)) * scale_hidden
    return (partial_dx, jnp.concatenate([grad_in, grad_down], axis=1))

def adam_update(old_weights, grad, first, second):
    first_new = beta_one * first + (1.0 - beta_one) * grad
    second_new = beta_two * second + (1.0 - beta_two) * grad * grad
    first_hat = first_new / (1.0 - beta_one ** adam_step)
    second_hat = second_new / (1.0 - beta_two ** adam_step)
    weight_f = old_weights.astype(jnp.float32)
    updated = weight_f - learn_rate * (first_hat / (jnp.sqrt(second_hat) + adam_eps) + decay_rate * weight_f)
    return (updated.astype(jnp.bfloat16), first_new, second_new)

def reference(tokens, expert_ids, gate_q, cotangent, placement, weights, moment_one, moment_two):
    expert_count = N_EXPERT
    group_count = N_DP
    capacity = CAP
    top_k = TOP
    tok_rows = TOK_DEV
    model_width = D
    hidden_units = HW
    slot_count = expert_count * capacity
    grouped_x = tokens.reshape(group_count, expert_count, tok_rows, model_width)
    grouped_ids = expert_ids.reshape(group_count, expert_count, tok_rows, top_k)
    grouped_q = gate_q.reshape(group_count, expert_count, tok_rows, top_k)
    grouped_dy = cotangent.reshape(group_count, expert_count, tok_rows, model_width)

    def group_step(total, group_item):
        rows_in, choices, gate_ints, cot_rows = group_item
        slots = jax.vmap(lambda one: slot_index(one, expert_count, capacity))(choices)
        inputs, scaled = jax.vmap(lambda a, b, c, d: fill_slots(a, b, c, d, slot_count, top_k))(rows_in, cot_rows, gate_ints, slots)
        inputs = inputs.reshape(expert_count, expert_count, capacity, model_width).transpose(1, 0, 2, 3).reshape(expert_count, expert_count * capacity, model_width)
        scaled = scaled.reshape(expert_count, expert_count, capacity, model_width).transpose(1, 0, 2, 3).reshape(expert_count, expert_count * capacity, model_width)
        partial_dx, group_grad = lax.map(lambda item: expert_pass(item[0], item[1], item[2]), (inputs, scaled, weights))
        partial_dx = partial_dx.reshape(expert_count, expert_count, capacity, model_width).transpose(1, 0, 2, 3).reshape(expert_count, slot_count, model_width)

        def collect(parts, slot_row):
            picked = parts[slot_row].astype(jnp.float32).reshape(tok_rows, top_k, model_width)
            return lax.optimization_barrier(jnp.sum(picked, axis=1)).astype(jnp.bfloat16)
        token_part = jax.vmap(collect)(partial_dx, slots)
        rounded = lax.optimization_barrier(group_grad.astype(jnp.bfloat16))
        return (total + rounded.astype(jnp.float32), token_part)
    start = jnp.zeros((expert_count, model_width, 3 * hidden_units), jnp.float32)
    grad, token_parts = lax.scan(group_step, start, (grouped_x, grouped_ids, grouped_q, grouped_dy))
    updated, first_new, second_new = adam_update(weights, grad, moment_one, moment_two)
    holder = jnp.zeros((expert_count,), jnp.int32).at[placement].set(jnp.arange(expert_count, dtype=jnp.int32))
    token_grad = token_parts.reshape(group_count * expert_count * tok_rows, model_width)
    return (token_grad, updated[holder], first_new[holder], second_new[holder])
```

```python
import functools

import jax
import jax.numpy as jnp
from jax import lax
from jax.experimental import pallas as pl
from jax.experimental.pallas import tpu as pltpu
from jax.sharding import PartitionSpec as P

beta_one = 0.9
beta_two = 0.95
learn_rate = 0.02
decay_rate = 0.1
adam_eps = 1e-08
adam_step = 20.0

MESH = pl.DeviceIdType.MESH
ANY = pl.BlockSpec(memory_space=pl.ANY)
VMEM = pl.BlockSpec(memory_space=pltpu.VMEM)

ORDER = (0, 1, 2, 3, 6, 7, 4, 5)
BATCHES = ((0, 1), (2, 3, 6, 7), (4, 5))


def coords():
    dp = lax.axis_index("dp")
    e = lax.axis_index("expert")
    return dp, e, e // 4, (e // 2) % 2, e % 2


def peer(dy, dl, dc):
    dp, _, y, l, c = coords()
    y2 = (y + dy) % 4 if dy else y
    l2 = 1 - l if dl else l
    c2 = 1 - c if dc else c
    return (dp, y2 * 4 + l2 * 2 + c2)


def dispatch_kernel(
    scales,
    tok,
    cot,
    pack,
    w,
    x_out,
    c_out,
    ha_out,
    p_out,
    gathered,
    ids,
    mrow,
    grow,
    gcol,
    onehot,
    wv,
    stage,
    xc,
    pre,
    ha,
    psend,
    precv,
    send,
    recv,
    local,
    outs,
):
    scale_w, scale_h = scales
    _, me, _, _, _ = coords()
    half, cap = 64, 56
    pair = 2 * cap
    hid = pre.shape[1] // 2
    others = [(dy, dl, dc) for dy in range(4) for dl in range(2) for dc in range(2)][1:]

    barrier = pltpu.get_barrier_semaphore()
    for o in others:
        pl.semaphore_signal(barrier, inc=1, device_id=peer(*o), device_id_type=MESH)
    pl.semaphore_wait(barrier, len(others))

    packs = []
    for n, (dy, dl, dc) in enumerate(others):
        seen = ((4 - dy) % 4) * 2 + dl
        packs.append(
            pltpu.make_async_remote_copy(
                src_ref=pack,
                dst_ref=ids.at[2 * seen + dc],
                send_sem=psend.at[n],
                recv_sem=precv.at[n],
                device_id=peer(dy, dl, dc),
                device_id_type=MESH,
            )
        )
    for d in packs:
        d.start()

    flight = {}

    def go(i, key, src, r, rows, to):
        n = len(flight)
        d = pltpu.make_async_remote_copy(
            src_ref=src,
            dst_ref=gathered.at[i, r, pl.ds(128 * to[2] + rows[0], rows[1] - rows[0])],
            send_sem=send.at[n],
            recv_sem=recv.at[n],
            device_id=peer(*to),
            device_id_type=MESH,
        )
        d.start()
        flight[(i, key)] = d

    UP, DOWN, ACROSS, SIB = (1, 0, 0), (3, 0, 0), (0, 1, 0), (0, 0, 1)
    own = (tok, cot)

    def mine(i, lo, hi):
        return own[i].at[pl.ds(lo, hi - lo)]

    def got(i, r, lo, hi):
        return gathered.at[i, r, pl.ds(lo, hi - lo)]

    def share(i, r, lo, hi):
        go(i, ("S", r, lo), got(i, r, lo, hi), r, (lo, hi), SIB)

    def land(i, key):
        flight[(i, key)].wait_recv()

    def first(i):
        go(i, "A1", mine(i, 0, 64), 1, (0, 64), ACROSS)
        go(i, "A2p0", mine(i, 0, 64), 6, (0, 64), UP)
        go(i, "A2m0", mine(i, 0, 64), 2, (0, 64), DOWN)
        go(i, "B1p", mine(i, 64, 128), 6, (64, 128), UP)
        go(i, "B1m", mine(i, 64, 128), 2, (64, 128), DOWN)
        go(i, "B30", mine(i, 64, 128), 1, (64, 128), ACROSS)
        go(i, ("S", 0, 0), own[i], 0, (0, 128), SIB)

    def second(i):
        land(i, "A1")
        go(i, "A2p1", got(i, 1, 0, 64), 7, (0, 64), UP)
        go(i, "A2m1", got(i, 1, 0, 64), 3, (0, 64), DOWN)
        share(i, 1, 0, 64)
        land(i, "A2p0")
        go(i, "A3p0", got(i, 6, 0, 32), 4, (0, 32), UP)
        share(i, 6, 0, 64)
        land(i, "A2m0")
        go(i, "A3m0", got(i, 2, 32, 64), 4, (32, 64), DOWN)
        share(i, 2, 0, 64)

    def third(i):
        land(i, "B1p")
        go(i, "B33", got(i, 6, 64, 128), 7, (64, 128), ACROSS)
        go(i, "B2p", got(i, 6, 64, 96), 4, (64, 96), UP)
        share(i, 6, 64, 128)
        land(i, "B1m")
        go(i, "B31", got(i, 2, 64, 128), 3, (64, 128), ACROSS)
        go(i, "B2m", got(i, 2, 96, 128), 4, (96, 128), DOWN)
        share(i, 2, 64, 128)
        land(i, "B30")
        share(i, 1, 64, 128)

    def fourth(i):
        land(i, "A2p1")
        go(i, "A3p1", got(i, 7, 0, 32), 5, (0, 32), UP)
        share(i, 7, 0, 64)
        land(i, "A2m1")
        go(i, "A3m1", got(i, 3, 32, 64), 5, (32, 64), DOWN)
        share(i, 3, 0, 64)
        land(i, "B2p")
        land(i, "B2m")
        go(i, "B32", got(i, 4, 64, 128), 5, (64, 128), ACROSS)
        land(i, "A3p0")
        land(i, "A3m0")
        share(i, 4, 0, 64)
        share(i, 4, 64, 128)
        land(i, "B33")
        share(i, 7, 64, 128)
        land(i, "B31")
        share(i, 3, 64, 128)

    def fifth(i):
        land(i, "A3p1")
        land(i, "A3m1")
        share(i, 5, 0, 64)
        land(i, "B32")
        share(i, 5, 64, 128)

    def fetch(i, batch):
        copies = []
        for n, r in enumerate(batch):
            if r == 0:
                land(i, ("S", 0, 0))
                copies.append(pltpu.make_async_copy(own[i], stage.at[n, pl.ds(0, 128)], local.at[n]))
                copies.append(
                    pltpu.make_async_copy(
                        gathered.at[i, 0, pl.ds(128, 128)], stage.at[n, pl.ds(128, 128)], local.at[4]
                    )
                )
            else:
                land(i, ("S", r, 0))
                land(i, ("S", r, 64))
                copies.append(pltpu.make_async_copy(gathered.at[i, r], stage.at[n], local.at[n]))
        for d in copies:
            d.start()
        for d in copies:
            d.wait()

    def pick(i, batch):
        fetch(i, batch)
        for n, r in enumerate(batch):
            at = ORDER.index(r) * pair
            rows = jnp.dot(onehot[r], stage[n], preferred_element_type=jnp.float32)
            if i == 1:
                rows = rows * gcol[pl.ds(at, pair), :]
            xc[i, pl.ds(at, pair), :] = rows.astype(jnp.bfloat16)

    def span(batch):
        return ORDER.index(batch[0]) * pair, len(batch) * pair

    def forward(batch):
        at, size = span(batch)
        wide = 512

        @pl.loop(0, 2 * hid // wide)
        def _(n):
            cols = pl.ds(pl.multiple_of(n * wide, wide), wide)
            pre[pl.ds(at, size), cols] = (
                jnp.dot(xc[0, pl.ds(at, size), :], wv[:, cols], preferred_element_type=jnp.float32)
                * scale_w
            )

    def backward(batch):
        at, size = span(batch)
        wide = 256

        @pl.loop(0, hid // wide)
        def _(n):
            def cols(start):
                return pl.ds(pl.multiple_of(start + n * wide, wide), wide)

            rows = pl.ds(at, size)
            da = (
                jnp.dot(xc[1, rows, :], wv[:, cols(2 * hid)], preferred_element_type=jnp.float32)
                * scale_h
            )
            gate = pre[rows, cols(0)]
            up = pre[rows, cols(hid)]
            sig = jax.nn.sigmoid(gate)
            gs = gate * sig
            ha[rows, cols(0)] = (da * up * sig * (1.0 + gate * (1.0 - sig))).astype(jnp.bfloat16)
            ha[rows, cols(hid)] = (da * gs).astype(jnp.bfloat16)
            ha[rows, cols(2 * hid)] = (gs * up).astype(jnp.bfloat16)

    first(0)
    weights_in = pltpu.make_async_copy(w, wv, local.at[5])
    weights_in.start()
    for d in packs:
        d.wait_recv()
    ids[0] = pack[...]
    for s in range(16):
        chosen = ids[s, 0:8, :] == me
        mrow[s : s + 1, :] = jnp.sum(
            jnp.where(chosen, 1.0, 0.0), axis=0, keepdims=True
        )
        grow[s : s + 1, :] = jnp.sum(
            jnp.where(chosen, ids[s, 8:16, :].astype(jnp.float32), 0.0), axis=0, keepdims=True
        ) * (1.0 / 65536.0)
    second(0)
    before = (
        lax.broadcasted_iota(jnp.int32, (128, 128), 0) < lax.broadcasted_iota(jnp.int32, (128, 128), 1)
    ).astype(jnp.bfloat16)
    position = jnp.dot(mrow[...].astype(jnp.bfloat16), before, preferred_element_type=jnp.float32)
    mrow[...] = jnp.where(mrow[...] > 0.5, position, -1000.0)
    slot = lax.broadcasted_iota(jnp.int32, (pair, 256), 0).astype(jnp.float32)
    for r in range(8):
        place = jnp.concatenate([mrow[2 * r : 2 * r + 1, :], mrow[2 * r + 1 : 2 * r + 2, :] + cap], axis=1)
        gate_row = jnp.concatenate([grow[2 * r : 2 * r + 1, :], grow[2 * r + 1 : 2 * r + 2, :]], axis=1)
        hit = jnp.where(slot == place, 1.0, 0.0)
        onehot[r] = hit.astype(jnp.bfloat16)
        gcol[pl.ds(ORDER.index(r) * pair, pair), :] = jnp.sum(hit * gate_row, axis=1, keepdims=True)
    third(0)
    first(1)
    fourth(0)
    pick(0, BATCHES[0])
    second(1)
    weights_in.wait()
    forward(BATCHES[0])
    fifth(0)
    third(1)
    pick(0, BATCHES[1])
    forward(BATCHES[1])
    fourth(1)
    pick(0, BATCHES[2])
    forward(BATCHES[2])
    done = [pltpu.make_async_copy(xc.at[0], x_out, outs.at[0]), pltpu.make_async_copy(onehot, p_out, outs.at[1])]
    for d in done:
        d.start()
    pick(1, BATCHES[0])
    backward(BATCHES[0])
    fifth(1)
    pick(1, BATCHES[1])
    backward(BATCHES[1])
    pick(1, BATCHES[2])
    backward(BATCHES[2])
    last = [pltpu.make_async_copy(xc.at[1], c_out, outs.at[2]), pltpu.make_async_copy(ha, ha_out, outs.at[3])]
    for d in last:
        d.start()
    for d in packs:
        d.wait_send()
    for d in flight.values():
        d.wait_send()
    for d in done + last:
        d.wait()


def dispatch(tokens, cotangent, pack, weights, scales):
    width = tokens.shape[1]
    total = weights.shape[1]
    hid = total // 3
    slots = 896
    bf, f32 = jnp.bfloat16, jnp.float32
    sems = pltpu.SemaphoreType.DMA
    return pl.pallas_call(
        functools.partial(dispatch_kernel, scales),
        name="dispatch",
        out_shape=(
            jax.ShapeDtypeStruct((slots, width), bf),
            jax.ShapeDtypeStruct((slots, width), bf),
            jax.ShapeDtypeStruct((slots, total), bf),
            jax.ShapeDtypeStruct((8, 112, 256), bf),
            jax.ShapeDtypeStruct((2, 8, 256, width), bf),
        ),
        in_specs=[ANY, ANY, VMEM, ANY],
        out_specs=(ANY,) * 5,
        scratch_shapes=[
            pltpu.VMEM((16, 16, 128), jnp.int32),
            pltpu.VMEM((16, 128), f32),
            pltpu.VMEM((16, 128), f32),
            pltpu.VMEM((slots, 1), f32),
            pltpu.VMEM((8, 112, 256), bf),
            pltpu.VMEM((width, total), bf),
            pltpu.VMEM((4, 256, width), bf),
            pltpu.VMEM((2, slots, width), bf),
            pltpu.VMEM((slots, 2 * hid), f32),
            pltpu.VMEM((slots, total), bf),
            sems((15,)),
            sems((15,)),
            sems((64,)),
            sems((64,)),
            sems((6,)),
            sems((4,)),
        ],
        compiler_params=pltpu.CompilerParams(
            collective_id=1, has_side_effects=True, vmem_limit_bytes=60 * 2**20
        ),
    )(tokens, cotangent, pack, weights)


def reduce_kernel(
    scales,
    x_in,
    c_in,
    ha_in,
    p_in,
    w,
    m_in,
    v_in,
    tok_grad,
    m_out,
    v_out,
    w_got,
    m_got,
    v_got,
    xt,
    ha,
    onehot,
    raw,
    g_send,
    r1,
    r2,
    x_send,
    x_recv,
    m_stage,
    v_stage,
    m_new,
    v_new,
    m_send,
    v_send,
    w_stage,
    pick,
    s_send,
    s_own,
    s_recv,
    l_recv,
    l_own,
    l_send,
    y1,
    y2,
    y_send,
    t_out,
    far_send,
    far_recv,
    load,
    z_send,
    r1_sem,
    r2_sem,
    xs_sem,
    xr_sem,
    state,
    new_sem,
    ms_sem,
    mr_sem,
    ss_sem,
    sr_sem,
    ls_sem,
    lr_sem,
    ys_sem,
    yr_sem,
    t_sem,
):
    scale_w, scale_h = scales
    dp, e, y, l, c = coords()
    z, h = dp // 2, dp % 2
    bf, f32 = jnp.bfloat16, jnp.float32
    up_z = (((z + 1) % 4) * 2 + h, e)
    down_z = (((z + 3) % 4) * 2 + h, e)
    other_h = (z * 2 + 1 - h, e)
    far = peer(2, 0, 0)
    sib = peer(0, 0, 1)
    across = peer(0, 1, 0)
    up_y = peer(1, 0, 0)
    down_y = peer(3, 0, 0)

    n_chunk, n_col = 9, 5
    cw = 256
    dw = 512
    quarter, eighth = 640, 320
    hid2 = 1536
    pair = 112

    barrier = pltpu.get_barrier_semaphore()
    greet = [up_z, down_z, other_h, far, sib, across, up_y, down_y]
    for d in greet:
        pl.semaphore_signal(barrier, inc=1, device_id=d, device_id_type=MESH)
    loads = [
        pltpu.make_async_copy(ha_in, ha, load.at[0]),
        pltpu.make_async_copy(p_in, onehot, load.at[1]),
    ]
    for d in loads:
        d.start()

    def raw_copy(i, q, slot):
        src = c_in if i else x_in
        start = pl.multiple_of(((z + q) % 4) * quarter, quarter)
        return pltpu.make_async_copy(src.at[:, pl.ds(start, quarter)], raw.at[slot], load.at[2 + slot])

    raw_copy(0, 2, 0).start()
    raw_copy(0, 1, 1).start()
    pl.semaphore_wait(barrier, len(greet))

    def remote(src, dst, ssem, rsem, to):
        return pltpu.make_async_remote_copy(
            src_ref=src, dst_ref=dst, send_sem=ssem, recv_sem=rsem, device_id=to, device_id_type=MESH
        )

    own_rows = pl.ds(pl.multiple_of(dp * eighth, eighth), eighth)
    far_w = remote(w.at[own_rows], w_got, far_send, far_recv, far)

    def turn(i, q, slot):
        raw_copy(i, q, slot).wait()
        for j in range(quarter // 128):
            xt[i, q, pl.ds(j * 128, 128), :] = raw[slot, :, pl.ds(j * 128, 128)].T

    turn(0, 2, 0)
    raw_copy(0, 3, 0).start()
    turn(0, 1, 1)
    raw_copy(0, 0, 1).start()
    loads[0].wait()
    turn(0, 3, 0)
    turn(0, 0, 1)
    loads[1].wait()
    raw_copy(1, 2, 0).start()
    raw_copy(1, 1, 1).start()
    turn(1, 2, 0)
    raw_copy(1, 3, 0).start()
    turn(1, 1, 1)
    raw_copy(1, 0, 1).start()
    turn(1, 3, 0)
    turn(1, 0, 1)

    def cols(k):
        return pl.ds(pl.multiple_of(k * cw, cw), cw)

    def product(k, q):
        scale = jnp.where(k < 6, scale_w, scale_h).astype(f32)
        return (
            jnp.dot(xt[k // 6, q], ha[:, cols(k)], preferred_element_type=f32) * scale
        )

    lo, hi = pl.ds(0, eighth), pl.ds(eighth, eighth)

    def z_copy(k, n):
        s = k % 3
        src = (
            g_send.at[s, 1, lo],
            g_send.at[s, 1, hi],
            g_send.at[s, 0, hi],
            g_send.at[s, 2, lo],
            g_send.at[s, 0, lo],
            g_send.at[s, 2, hi],
        )[n]
        dst = (
            r1.at[k, 0],
            r1.at[k, 1],
            r2.at[k, 0, hi],
            r2.at[k, 1, lo],
            r2.at[k, 0, lo],
            r2.at[k, 1, hi],
        )[n]
        rsem = (r1_sem.at[k, 0], r1_sem.at[k, 1], r2_sem.at[k, 0], r2_sem.at[k, 1], r2_sem.at[k, 2], r2_sem.at[k, 3])[n]
        return remote(src, dst, z_send.at[s, n], rsem, up_z if n % 2 == 0 else down_z)

    def h_copy(k):
        return remote(x_send.at[k % 2], x_recv.at[k], xs_sem.at[k % 2], xr_sem.at[k], other_h)

    def m_copy(k, n):
        src = (m_send, v_send)[n].at[k % 2]
        dst = (m_got, v_got)[n].at[:, cols(k)]
        return remote(src, dst, ms_sem.at[k % 2, n], mr_sem.at[k, n], far)

    def state_in(k, n):
        return pltpu.make_async_copy((m_in, v_in)[n].at[:, cols(k)], (m_stage, v_stage)[n].at[k % 2], state.at[k % 2, n])

    def state_out(k, n):
        return pltpu.make_async_copy((m_new, v_new)[n].at[k % 2], (m_out, v_out)[n].at[:, cols(k)], new_sem.at[k % 2, n])

    def grads(k):
        @pl.when(k >= 3)
        def _():
            for n in range(6):
                z_copy(k - 3, n).wait_send()

        s = k % 3
        g_send[s, 1] = product(k, 2).astype(bf)
        z_copy(k, 0).start()
        z_copy(k, 1).start()
        g_send[s, 0] = product(k, 1).astype(bf)
        z_copy(k, 2).start()
        g_send[s, 2] = product(k, 3).astype(bf)
        z_copy(k, 3).start()

    def relay(k):
        s = k % 3
        z_copy(k, 0).wait_recv()
        g_send[s, 0, lo] = (g_send[s, 0, lo].astype(f32) + r1[k, 0].astype(f32)).astype(bf)
        z_copy(k, 4).start()
        z_copy(k, 1).wait_recv()
        g_send[s, 2, hi] = (g_send[s, 2, hi].astype(f32) + r1[k, 1].astype(f32)).astype(bf)
        z_copy(k, 5).start()

    def gather_z(k):
        own = product(k, 0)
        for n in (2, 3, 4, 5):
            z_copy(k, n).wait_recv()
        raw_sum = own + r2[k, 0].astype(f32) + r2[k, 1].astype(f32)

        @pl.when(k >= 2)
        def _():
            h_copy(k - 2).wait_send()

        mine_first = h == 0
        x_send[k % 2] = jnp.where(mine_first, raw_sum[eighth:], raw_sum[:eighth]).astype(bf)
        h_copy(k).start()
        pick[k % 2] = jnp.where(mine_first, raw_sum[:eighth], raw_sum[eighth:])
        for n in range(2):
            state_in(k, n).start()

    def adam(k):
        h_copy(k).wait_recv()
        g = pick[k % 2] + x_recv[k].astype(f32)
        for n in range(2):
            state_in(k, n).wait()

        @pl.when(k >= 2)
        def _():
            for n in range(2):
                m_copy(k - 2, n).wait_send()
                state_out(k - 2, n).wait()

        s = k % 2
        m1 = beta_one * m_stage[s] + (1.0 - beta_one) * g
        v1 = beta_two * v_stage[s] + (1.0 - beta_two) * g * g
        m_new[s] = m1
        v_new[s] = v1
        m_send[s] = m1.astype(bf)
        v_send[s] = v1.astype(bf)
        for n in range(2):
            m_copy(k, n).start()
            state_out(k, n).start()

    def wide(j):
        return pl.ds(pl.multiple_of(j * dw, dw), dw)

    def w_copy(j):
        rows = pl.ds(pl.multiple_of(j * dw, dw), dw)
        return pltpu.make_async_copy(w.at[rows, pl.ds(0, hid2)], w_stage, load.at[4])

    def s_copy(j):
        return remote(s_send.at[j % 2], s_recv.at[j], ss_sem.at[j % 2], sr_sem.at[j], sib)

    def l_copy(j):
        return remote(l_send.at[j % 2], l_recv.at[j], ls_sem.at[j % 2], lr_sem.at[j], across)

    def y_copy(j, n):
        b = j % 2
        src = (l_own.at[j, 2, pl.ds(0, 64)], l_own.at[j, 2, pl.ds(64, 64)], y_send.at[b, 0], y_send.at[b, 1])[n]
        dst = (y1.at[j, 0], y1.at[j, 1], y2.at[j, 0], y2.at[j, 1])[n]
        return remote(src, dst, ys_sem.at[b, n], yr_sem.at[j, n], up_y if n % 2 == 0 else down_y)

    def t_copy(j):
        return pltpu.make_async_copy(t_out.at[j % 2], tok_grad.at[:, wide(j)], t_sem.at[j % 2])

    def inputs_back(j):
        w_copy(j).wait()

        @pl.when(j >= 2)
        def _():
            s_copy(j - 2).wait_send()

        b = j % 2
        dx = (
            lax.dot_general(
                ha[:, pl.ds(0, hid2)], w_stage[...], (((1,), (1,)), ((), ())), preferred_element_type=f32
            )
            * scale_w
        ).astype(bf)
        for r in range(8):
            at = ORDER.index(r) * pair
            back = lax.dot_general(
                onehot[r], dx[at : at + pair], (((0,), (0,)), ((), ())), preferred_element_type=f32
            ).astype(bf)
            s_own[b, r] = back[:128]
            s_send[b, r] = back[128:]
        s_copy(j).start()

        @pl.when(j + 1 < n_col)
        def _():
            w_copy(j + 1).start()

    def add_core(j):
        b = j % 2
        s_copy(j).wait_recv()

        @pl.when(j >= 2)
        def _():
            l_copy(j - 2).wait_send()

        for dy in range(4):
            l_send[b, dy] = (s_own[b, 2 * dy + 1].astype(f32) + s_recv[j, 2 * dy + 1].astype(f32)).astype(bf)
        l_copy(j).start()
        for dy in range(4):
            l_own[j, dy] = (s_own[b, 2 * dy].astype(f32) + s_recv[j, 2 * dy].astype(f32)).astype(bf)

    def add_across(j):
        l_copy(j).wait_recv()
        for dy in (2, 1, 3, 0):
            l_own[j, dy] = (l_own[j, dy].astype(f32) + l_recv[j, dy].astype(f32)).astype(bf)
        y_copy(j, 0).start()
        y_copy(j, 1).start()

    def add_relay(j):
        b = j % 2
        top, low = pl.ds(0, 64), pl.ds(64, 64)
        y_copy(j, 0).wait_recv()
        y_copy(j, 1).wait_recv()

        @pl.when(j >= 2)
        def _():
            for n in range(4):
                y_copy(j - 2, n).wait_send()

        y_send[b, 0, top] = (l_own[j, 1, top].astype(f32) + y1[j, 0].astype(f32)).astype(bf)
        y_send[b, 0, low] = l_own[j, 1, low]
        y_send[b, 1, top] = l_own[j, 3, top]
        y_send[b, 1, low] = (l_own[j, 3, low].astype(f32) + y1[j, 1].astype(f32)).astype(bf)
        y_copy(j, 2).start()
        y_copy(j, 3).start()

    def add_last(j):
        @pl.when(j >= 2)
        def _():
            t_copy(j - 2).wait()

        b = j % 2

        y_copy(j, 2).wait_recv()
        y_copy(j, 3).wait_recv()
        t_out[b] = (l_own[j, 0].astype(f32) + y2[j, 0].astype(f32) + y2[j, 1].astype(f32)).astype(bf)
        t_copy(j).start()

    w_copy(0).start()

    def stage(t, delay, count, body):
        k = t - delay

        @pl.when((k >= 0) & (k < count))
        def _():
            body(k)

    @pl.loop(0, n_chunk + 4)
    def _(t):
        stage(t, 0, n_chunk, grads)

        @pl.when(t == 0)
        def _():
            far_w.start()

        stage(t, 4, n_chunk, adam)
        stage(t, 0, n_col, inputs_back)
        stage(t, 1, n_chunk, relay)
        stage(t, 1, n_col, add_core)
        stage(t, 2, n_col, add_across)
        stage(t, 3, n_col, add_relay)
        stage(t, 3, n_chunk, gather_z)
        stage(t, 4, n_col, add_last)

    for k in range(n_chunk - 3, n_chunk):
        for n in range(6):
            z_copy(k, n).wait_send()
    for k in range(n_chunk - 2, n_chunk):
        h_copy(k).wait_send()
        for n in range(2):
            m_copy(k, n).wait_send()
            state_out(k, n).wait()
    for j in range(n_col - 2, n_col):
        s_copy(j).wait_send()
        l_copy(j).wait_send()
        for n in range(4):
            y_copy(j, n).wait_send()
        t_copy(j).wait()
    far_w.wait()
    for k in range(n_chunk):
        for n in range(2):
            m_copy(k, n).wait_recv()


def reduce(x, cots, ha, onehot, weights, moment_one, moment_two, scales):
    width, total = weights.shape
    rows = moment_one.shape[0]
    bf, f32 = jnp.bfloat16, jnp.float32
    sems = pltpu.SemaphoreType.DMA
    small = jax.ShapeDtypeStruct((rows, total), bf)
    large = jax.ShapeDtypeStruct((rows, total), f32)
    return pl.pallas_call(
        functools.partial(reduce_kernel, scales),
        name="reduce",
        out_shape=(jax.ShapeDtypeStruct((128, width), bf), large, large, small, small, small),
        in_specs=[ANY] * 7,
        out_specs=(ANY,) * 6,
        scratch_shapes=[
            pltpu.VMEM((2, 4, 640, 896), bf),
            pltpu.VMEM((896, 2304), bf),
            pltpu.VMEM((8, 112, 256), bf),
            pltpu.VMEM((2, 896, 640), bf),
            pltpu.VMEM((3, 3, 640, 256), bf),
            pltpu.VMEM((9, 2, 320, 256), bf),
            pltpu.VMEM((9, 2, 640, 256), bf),
            pltpu.VMEM((2, 320, 256), bf),
            pltpu.VMEM((9, 320, 256), bf),
            pltpu.VMEM((2, 320, 256), f32),
            pltpu.VMEM((2, 320, 256), f32),
            pltpu.VMEM((2, 320, 256), f32),
            pltpu.VMEM((2, 320, 256), f32),
            pltpu.VMEM((2, 320, 256), bf),
            pltpu.VMEM((2, 320, 256), bf),
            pltpu.VMEM((512, 1536), bf),
            pltpu.VMEM((2, 320, 256), f32),
            pltpu.VMEM((2, 8, 128, 512), bf),
            pltpu.VMEM((2, 8, 128, 512), bf),
            pltpu.VMEM((5, 8, 128, 512), bf),
            pltpu.VMEM((5, 4, 128, 512), bf),
            pltpu.VMEM((5, 4, 128, 512), bf),
            pltpu.VMEM((2, 4, 128, 512), bf),
            pltpu.VMEM((5, 2, 64, 512), bf),
            pltpu.VMEM((5, 2, 128, 512), bf),
            pltpu.VMEM((2, 2, 128, 512), bf),
            pltpu.VMEM((2, 128, 512), bf),
            sems(()),
            sems(()),
            sems((5,)),
            sems((3, 6)),
            sems((9, 2)),
            sems((9, 4)),
            sems((2,)),
            sems((9,)),
            sems((2, 2)),
            sems((2, 2)),
            sems((2, 2)),
            sems((9, 2)),
            sems((2,)),
            sems((5,)),
            sems((2,)),
            sems((5,)),
            sems((2, 4)),
            sems((5, 4)),
            sems((2,)),
        ],
        compiler_params=pltpu.CompilerParams(
            collective_id=2, has_side_effects=True, vmem_limit_bytes=60 * 2**20
        ),
    )(x, cots, ha, onehot, weights, moment_one, moment_two)


def place_kernel(info, w, w_got, m_own, v_own, m_got, v_got, w_new, m_new, v_new):
    def write(rows, first, second):
        weight = rows.astype(jnp.float32)
        first_hat = first * (1.0 / (1.0 - beta_one**adam_step))
        second_hat = second * (1.0 / (1.0 - beta_two**adam_step))
        m_new[0] = first
        v_new[0] = second
        w_new[0] = (
            weight - learn_rate * (first_hat / (jnp.sqrt(second_hat) + adam_eps) + decay_rate * weight)
        ).astype(w_new.dtype)

    @pl.when(info[0] == 0)
    def _():
        write(w[...], m_own[...], v_own[...])

    @pl.when(info[0] != 0)
    def _():
        write(w_got[...], m_got[...].astype(jnp.float32), v_got[...].astype(jnp.float32))


def place(info, weights, w_got, m_own, v_own, m_got, v_got):
    rows, total = m_own.shape
    step = 64
    steps = rows // step
    stay = pl.BlockSpec((step, total), lambda i, f: (jnp.where(f[0] == 0, i, 0), 0))
    move = pl.BlockSpec((step, total), lambda i, f: (jnp.where(f[0] == 0, 0, i), 0))
    old = pl.BlockSpec((step, total), lambda i, f: (f[1] * steps + jnp.where(f[0] == 0, i, 0), 0))
    out = pl.BlockSpec((1, step, total), lambda i, f: (0, i, 0))
    return pl.pallas_call(
        place_kernel,
        name="place",
        grid_spec=pltpu.PrefetchScalarGridSpec(
            num_scalar_prefetch=1,
            grid=(steps,),
            in_specs=[old, move, stay, stay, move, move],
            out_specs=(out, out, out),
        ),
        out_shape=(
            jax.ShapeDtypeStruct((1, rows, total), jnp.bfloat16),
            jax.ShapeDtypeStruct((1, rows, total), jnp.float32),
            jax.ShapeDtypeStruct((1, rows, total), jnp.float32),
        ),
        compiler_params=pltpu.CompilerParams(vmem_limit_bytes=40 * 2**20),
    )(info, weights, w_got, m_own, v_own, m_got, v_got)


def shards(tokens, expert_ids, gate_q, cotangent, placement, weights, moment_one, moment_two):
    my_slot = lax.axis_index("expert")
    dp_index = lax.axis_index("dp")
    width = tokens.shape[1]
    hidden = weights.shape[2] // 3
    scales = (width ** (-0.5), hidden ** (-0.5))
    pack = jnp.concatenate(
        [
            jnp.pad(expert_ids.T, ((0, 2), (0, 0)), constant_values=-1),
            jnp.pad(gate_q.T, ((0, 2), (0, 0))),
        ],
        axis=0,
    )
    x, cots, ha, onehot, _ = dispatch(tokens, cotangent, pack, weights[0], scales)
    token_grad, m_own, v_own, w_got, m_got, v_got = reduce(
        x, cots, ha, onehot, weights[0], moment_one[0], moment_two[0], scales
    )
    moving = (placement[my_slot] != my_slot).astype(jnp.int32)
    info = jnp.stack([moving, dp_index.astype(jnp.int32)])
    new_w, new_m, new_v = place(info, weights[0], w_got, m_own, v_own, m_got, v_got)
    return (token_grad, new_w, new_m, new_v)


def solution(mesh):
    placed = (
        P(("dp", "expert"), None),
        P(("dp", "expert"), None),
        P(("dp", "expert"), None),
        P(("dp", "expert"), None),
        P(),
        P("expert", None, None),
        P("expert", "dp", None),
        P("expert", "dp", None),
    )
    return jax.shard_map(
        shards,
        mesh=mesh,
        in_specs=placed,
        out_specs=(
            P(("dp", "expert"), None),
            P("expert", "dp", None),
            P("expert", "dp", None),
            P("expert", "dp", None),
        ),
        check_vma=False,
    )
```

```python
import functools

import jax
import jax.numpy as jnp
from jax import lax
from jax.experimental import pallas as pl
from jax.experimental.pallas import tpu as pltpu
from jax.sharding import PartitionSpec as P

beta_one = 0.9
beta_two = 0.95
learn_rate = 0.02
decay_rate = 0.1
adam_eps = 1e-08
adam_step = 20.0

MESH = pl.DeviceIdType.MESH
ANY = pl.BlockSpec(memory_space=pl.ANY)
VMEM = pl.BlockSpec(memory_space=pltpu.VMEM)

ORDER = (0, 1, 2, 3, 6, 7, 4, 5)
BATCHES = ((0, 1), (2, 3, 6, 7), (4, 5))


def coords():
    dp = lax.axis_index("dp")
    e = lax.axis_index("expert")
    return dp, e, e // 4, (e // 2) % 2, e % 2


def peer(dy, dl, dc):
    dp, _, y, l, c = coords()
    y2 = (y + dy) % 4 if dy else y
    l2 = 1 - l if dl else l
    c2 = 1 - c if dc else c
    return (dp, y2 * 4 + l2 * 2 + c2)


def dispatch_kernel(
    scales,
    tok,
    cot,
    pack,
    w,
    xt_out,
    ha_out,
    p_out,
    gathered,
    ids,
    mrow,
    grow,
    gcol,
    onehot,
    wv,
    stage,
    xc,
    xt,
    pre,
    ha,
    psend,
    precv,
    send,
    recv,
    local,
    outs,
):
    scale_w, scale_h = scales
    _, me, _, _, _ = coords()
    cap, pair = 56, 128
    hid = pre.shape[1] // 2
    chips = [(dy, dl, 0) for dy in range(4) for dl in range(2)][1:]
    others = chips + [(0, 0, 1)]

    barrier = pltpu.get_barrier_semaphore()
    for o in others:
        pl.semaphore_signal(barrier, inc=1, device_id=peer(*o), device_id_type=MESH)
    pl.semaphore_wait(barrier, len(others))

    packs = []
    for n, (dy, dl, dc) in enumerate(chips):
        packs.append(
            pltpu.make_async_remote_copy(
                src_ref=pack,
                dst_ref=ids.at[0, ((4 - dy) % 4) * 2 + dl],
                send_sem=psend.at[n],
                recv_sem=precv.at[n],
                device_id=peer(dy, dl, dc),
                device_id_type=MESH,
            )
        )
    for d in packs:
        d.start()
    ids[0, 0] = pack[...]

    flight = {}

    def go(i, key, src, r, rows, to):
        n = len(flight)
        d = pltpu.make_async_remote_copy(
            src_ref=src,
            dst_ref=gathered.at[i, r, pl.ds(128 * to[2] + rows[0], rows[1] - rows[0])],
            send_sem=send.at[n],
            recv_sem=recv.at[n],
            device_id=peer(*to),
            device_id_type=MESH,
        )
        d.start()
        flight[(i, key)] = d

    UP, DOWN, ACROSS, SIB = (1, 0, 0), (3, 0, 0), (0, 1, 0), (0, 0, 1)
    own = (tok, cot)

    def mine(i, lo, hi):
        return own[i].at[pl.ds(lo, hi - lo)]

    def got(i, r, lo, hi):
        return gathered.at[i, r, pl.ds(lo, hi - lo)]

    def share(i, r, lo, hi):
        go(i, ("S", r, lo), got(i, r, lo, hi), r, (lo, hi), SIB)

    def land(i, key):
        flight[(i, key)].wait_recv()

    cut = (80, 64)
    fork = ((48, 32), (32, 32))
    fork_b = (96, 96)

    def first(i):
        a = cut[i]
        go(i, "A1", mine(i, 0, a), 1, (0, a), ACROSS)
        go(i, "B1p", mine(i, a, 128), 6, (a, 128), UP)
        go(i, "B1m", mine(i, a, 128), 2, (a, 128), DOWN)
        go(i, "A2p0", mine(i, 0, a), 6, (0, a), UP)
        go(i, "A2m0", mine(i, 0, a), 2, (0, a), DOWN)
        go(i, "B30", mine(i, a, 128), 1, (a, 128), ACROSS)
        go(i, ("S", 0, 0), own[i], 0, (0, 128), SIB)

    def second(i):
        a, f = cut[i], fork[i][0]
        land(i, "A1")
        go(i, "A2p1", got(i, 1, 0, a), 7, (0, a), UP)
        go(i, "A2m1", got(i, 1, 0, a), 3, (0, a), DOWN)
        share(i, 1, 0, a)
        land(i, "A2p0")
        go(i, "A3p0", got(i, 6, 0, f), 4, (0, f), UP)
        share(i, 6, 0, a)
        land(i, "A2m0")
        go(i, "A3m0", got(i, 2, f, a), 4, (f, a), DOWN)
        share(i, 2, 0, a)

    def third(i):
        a, b = cut[i], fork_b[i]
        land(i, "B1p")
        go(i, "B33", got(i, 6, a, 128), 7, (a, 128), ACROSS)
        go(i, "B2p", got(i, 6, a, b), 4, (a, b), UP)
        share(i, 6, a, 128)
        land(i, "B1m")
        go(i, "B31", got(i, 2, a, 128), 3, (a, 128), ACROSS)
        go(i, "B2m", got(i, 2, b, 128), 4, (b, 128), DOWN)
        share(i, 2, a, 128)
        land(i, "B30")
        share(i, 1, a, 128)

    def fourth(i):
        a, f = cut[i], fork[i][1]
        land(i, "A2p1")
        go(i, "A3p1", got(i, 7, 0, f), 5, (0, f), UP)
        share(i, 7, 0, a)
        land(i, "A2m1")
        go(i, "A3m1", got(i, 3, f, a), 5, (f, a), DOWN)
        share(i, 3, 0, a)
        land(i, "B2p")
        land(i, "B2m")
        go(i, "B32", got(i, 4, a, 128), 5, (a, 128), ACROSS)
        land(i, "A3p0")
        land(i, "A3m0")
        share(i, 4, 0, a)
        share(i, 4, a, 128)
        land(i, "B33")
        share(i, 7, a, 128)
        land(i, "B31")
        share(i, 3, a, 128)

    def fifth(i):
        a = cut[i]
        land(i, "A3p1")
        land(i, "A3m1")
        share(i, 5, 0, a)
        land(i, "B32")
        share(i, 5, a, 128)

    def fetch(i, batch):
        copies = []
        for n, r in enumerate(batch):
            if r == 0:
                land(i, ("S", 0, 0))
                copies.append(pltpu.make_async_copy(own[i], stage.at[n, pl.ds(0, 128)], local.at[n]))
                copies.append(
                    pltpu.make_async_copy(
                        gathered.at[i, 0, pl.ds(128, 128)], stage.at[n, pl.ds(128, 128)], local.at[4]
                    )
                )
            else:
                land(i, ("S", r, 0))
                land(i, ("S", r, cut[i]))
                copies.append(pltpu.make_async_copy(gathered.at[i, r], stage.at[n], local.at[n]))
        for d in copies:
            d.start()
        for d in copies:
            d.wait()

    def pick(i, batch):
        fetch(i, batch)
        for n, r in enumerate(batch):
            at = ORDER.index(r) * pair
            rows = jnp.dot(onehot[r], stage[n], preferred_element_type=jnp.float32)
            if i == 1:
                rows = rows * gcol[pl.ds(at, pair), :]
            rows = rows.astype(jnp.bfloat16)
            xc[pl.ds(n * pair, pair), :] = rows
            for col in range(0, rows.shape[1], 128):
                xt[i, pl.ds(col, 128), pl.ds(at, pair)] = rows[:, col : col + 128].T
        at, size = span(batch)
        out(xt.at[i, :, pl.ds(at, size)], xt_out.at[i, :, pl.ds(at, size)])

    def out(src, dst):
        d = pltpu.make_async_copy(src, dst, outs.at[len(written)])
        d.start()
        written.append(d)

    written = []

    def span(batch):
        return ORDER.index(batch[0]) * pair, len(batch) * pair

    def forward(batch):
        at, size = span(batch)
        wide = 512

        @pl.loop(0, 2 * hid // wide)
        def _(n):
            cols = pl.ds(pl.multiple_of(n * wide, wide), wide)
            pre[pl.ds(at, size), cols] = (
                jnp.dot(xc[pl.ds(0, size), :], wv[:, cols], preferred_element_type=jnp.float32)
                * scale_w
            )

    def backward(batch):
        at, size = span(batch)
        wide = 256

        @pl.loop(0, hid // wide)
        def _(n):
            def cols(start):
                return pl.ds(pl.multiple_of(start + n * wide, wide), wide)

            rows = pl.ds(at, size)
            da = (
                jnp.dot(xc[pl.ds(0, size), :], wv[:, cols(2 * hid)], preferred_element_type=jnp.float32)
                * scale_h
            )
            gate = pre[rows, cols(0)]
            up = pre[rows, cols(hid)]
            sig = jax.nn.sigmoid(gate)
            gs = gate * sig
            ha[rows, cols(0)] = (da * up * sig * (1.0 + gate * (1.0 - sig))).astype(jnp.bfloat16)
            ha[rows, cols(hid)] = (da * gs).astype(jnp.bfloat16)
            ha[rows, cols(2 * hid)] = (gs * up).astype(jnp.bfloat16)

        out(ha.at[pl.ds(at, size)], ha_out.at[pl.ds(at, size)])

    first(0)
    weights_in = pltpu.make_async_copy(w, wv, local.at[5])
    weights_in.start()
    for d in packs:
        d.wait_recv()
    swap = pltpu.make_async_remote_copy(
        src_ref=ids.at[0],
        dst_ref=ids.at[1],
        send_sem=psend.at[7],
        recv_sem=precv.at[7],
        device_id=peer(*SIB),
        device_id_type=MESH,
    )
    swap.start()
    second(0)
    swap.wait_recv()
    for r in range(8):
        for core in range(2):
            s = 2 * r + core
            chosen = ids[core, r, 0:8, :] == me
            mrow[s : s + 1, :] = jnp.sum(jnp.where(chosen, 1.0, 0.0), axis=0, keepdims=True)
            grow[s : s + 1, :] = jnp.sum(
                jnp.where(chosen, ids[core, r, 8:16, :].astype(jnp.float32), 0.0), axis=0, keepdims=True
            ) * (1.0 / 65536.0)
    before = (
        lax.broadcasted_iota(jnp.int32, (128, 128), 0) < lax.broadcasted_iota(jnp.int32, (128, 128), 1)
    ).astype(jnp.bfloat16)
    position = jnp.dot(mrow[...].astype(jnp.bfloat16), before, preferred_element_type=jnp.float32)
    mrow[...] = jnp.where(mrow[...] > 0.5, position, -1000.0)
    slot = lax.broadcasted_iota(jnp.int32, (pair, 256), 0).astype(jnp.float32)
    for r in range(8):
        place = jnp.concatenate([mrow[2 * r : 2 * r + 1, :], mrow[2 * r + 1 : 2 * r + 2, :] + cap], axis=1)
        gate_row = jnp.concatenate([grow[2 * r : 2 * r + 1, :], grow[2 * r + 1 : 2 * r + 2, :]], axis=1)
        hit = jnp.where(slot == place, 1.0, 0.0)
        onehot[r] = hit.astype(jnp.bfloat16)
        gcol[pl.ds(ORDER.index(r) * pair, pair), :] = jnp.sum(hit * gate_row, axis=1, keepdims=True)
    out(onehot, p_out)
    third(0)
    first(1)
    pick(0, BATCHES[0])
    weights_in.wait()
    forward(BATCHES[0])
    fourth(0)
    second(1)
    pick(0, BATCHES[1])
    forward(BATCHES[1])
    fifth(0)
    third(1)
    pick(0, BATCHES[2])
    forward(BATCHES[2])
    pick(1, BATCHES[0])
    backward(BATCHES[0])
    fourth(1)
    pick(1, BATCHES[1])
    backward(BATCHES[1])
    fifth(1)
    pick(1, BATCHES[2])
    backward(BATCHES[2])
    for d in packs:
        d.wait_send()
    swap.wait_send()
    for d in flight.values():
        d.wait_send()
    for d in written:
        d.wait()


def dispatch(tokens, cotangent, pack, weights, scales):
    width = tokens.shape[1]
    total = weights.shape[1]
    hid = total // 3
    slots = 1024
    bf, f32 = jnp.bfloat16, jnp.float32
    sems = pltpu.SemaphoreType.DMA
    return pl.pallas_call(
        functools.partial(dispatch_kernel, scales),
        name="dispatch",
        out_shape=(
            jax.ShapeDtypeStruct((2, width, slots), bf),
            jax.ShapeDtypeStruct((slots, total), bf),
            jax.ShapeDtypeStruct((8, 128, 256), bf),
            jax.ShapeDtypeStruct((2, 8, 256, width), bf),
        ),
        in_specs=[ANY, ANY, VMEM, ANY],
        out_specs=(ANY,) * 4,
        scratch_shapes=[
            pltpu.VMEM((2, 8, 16, 128), jnp.int32),
            pltpu.VMEM((16, 128), f32),
            pltpu.VMEM((16, 128), f32),
            pltpu.VMEM((slots, 1), f32),
            pltpu.VMEM((8, 128, 256), bf),
            pltpu.VMEM((width, total), bf),
            pltpu.VMEM((4, 256, width), bf),
            pltpu.VMEM((512, width), bf),
            pltpu.VMEM((2, width, slots), bf),
            pltpu.VMEM((slots, 2 * hid), f32),
            pltpu.VMEM((slots, total), bf),
            sems((8,)),
            sems((8,)),
            sems((64,)),
            sems((64,)),
            sems((6,)),
            sems((10,)),
        ],
        compiler_params=pltpu.CompilerParams(
            collective_id=1, has_side_effects=True, vmem_limit_bytes=60 * 2**20
        ),
    )(tokens, cotangent, pack, weights)


def reduce_kernel(
    scales,
    xt_in,
    ha_in,
    p_in,
    w,
    m_in,
    v_in,
    tok_grad,
    m_out,
    v_out,
    w_got,
    m_got,
    v_got,
    xt,
    ha,
    onehot,
    g_send,
    r1,
    r2,
    x_send,
    x_recv,
    m_stage,
    v_stage,
    m_new,
    v_new,
    m_send,
    v_send,
    w_stage,
    pick,
    s_send,
    s_own,
    s_recv,
    l_recv,
    l_own,
    l_send,
    y1,
    y2,
    y_send,
    t_out,
    far_send,
    far_recv,
    load,
    z_send,
    r1_sem,
    r2_sem,
    xs_sem,
    xr_sem,
    state,
    new_sem,
    ms_sem,
    mr_sem,
    ss_sem,
    sr_sem,
    ls_sem,
    lr_sem,
    ys_sem,
    yr_sem,
    t_sem,
):
    scale_w, scale_h = scales
    dp, e, y, l, c = coords()
    z, h = dp // 2, dp % 2
    bf, f32 = jnp.bfloat16, jnp.float32
    up_z = (((z + 1) % 4) * 2 + h, e)
    down_z = (((z + 3) % 4) * 2 + h, e)
    other_h = (z * 2 + 1 - h, e)
    far = peer(2, 0, 0)
    sib = peer(0, 0, 1)
    across = peer(0, 1, 0)
    up_y = peer(1, 0, 0)
    down_y = peer(3, 0, 0)

    n_chunk, n_col = 9, 10
    cw = 256
    dw = 256
    quarter, eighth = 640, 320
    hid2 = 1536
    pair = 128

    barrier = pltpu.get_barrier_semaphore()
    greet = [up_z, down_z, other_h, far, sib, across, up_y, down_y]
    for d in greet:
        pl.semaphore_signal(barrier, inc=1, device_id=d, device_id_type=MESH)

    def rows_in(i, q):
        start = pl.multiple_of(((z + q) % 4) * quarter, quarter)
        return pltpu.make_async_copy(xt_in.at[i, pl.ds(start, quarter)], xt.at[i, q], load.at[4 * i + q])

    rows_in(0, 2).start()
    ha_load = pltpu.make_async_copy(ha_in, ha, load.at[8])
    ha_load.start()
    for q in (1, 3, 0):
        rows_in(0, q).start()
    onehot_load = pltpu.make_async_copy(p_in, onehot, load.at[9])
    onehot_load.start()
    for q in (2, 1, 3, 0):
        rows_in(1, q).start()
    pl.semaphore_wait(barrier, len(greet))

    def remote(src, dst, ssem, rsem, to):
        return pltpu.make_async_remote_copy(
            src_ref=src, dst_ref=dst, send_sem=ssem, recv_sem=rsem, device_id=to, device_id_type=MESH
        )

    own_rows = pl.ds(pl.multiple_of(dp * eighth, eighth), eighth)
    far_w = remote(w.at[own_rows], w_got, far_send, far_recv, far)

    def cols(k):
        return pl.ds(pl.multiple_of(k * cw, cw), cw)

    def product(k, q):
        scale = jnp.where(k < 6, scale_w, scale_h).astype(f32)
        return (
            jnp.dot(xt[k // 6, q], ha[:, cols(k)], preferred_element_type=f32) * scale
        )

    lo, hi = pl.ds(0, eighth), pl.ds(eighth, eighth)

    def z_copy(k, n):
        s = k % 3
        src = (
            g_send.at[s, 1, lo],
            g_send.at[s, 1, hi],
            g_send.at[s, 0, hi],
            g_send.at[s, 2, lo],
            g_send.at[s, 0, lo],
            g_send.at[s, 2, hi],
        )[n]
        dst = (
            r1.at[k, 0],
            r1.at[k, 1],
            r2.at[k, 0, hi],
            r2.at[k, 1, lo],
            r2.at[k, 0, lo],
            r2.at[k, 1, hi],
        )[n]
        rsem = (r1_sem.at[k, 0], r1_sem.at[k, 1], r2_sem.at[k, 0], r2_sem.at[k, 1], r2_sem.at[k, 2], r2_sem.at[k, 3])[n]
        return remote(src, dst, z_send.at[s, n], rsem, up_z if n % 2 == 0 else down_z)

    def h_copy(k):
        return remote(x_send.at[k % 3], x_recv.at[k], xs_sem.at[k % 3], xr_sem.at[k], other_h)

    def m_copy(k, n):
        src = (m_send, v_send)[n].at[k]
        dst = (m_got, v_got)[n].at[:, cols(k)]
        return remote(src, dst, ms_sem.at[k, n], mr_sem.at[k, n], far)

    def state_in(k, n):
        return pltpu.make_async_copy((m_in, v_in)[n].at[:, cols(k)], (m_stage, v_stage)[n].at[k % 3], state.at[k % 3, n])

    def state_out(k, n):
        return pltpu.make_async_copy((m_new, v_new)[n].at[k % 2], (m_out, v_out)[n].at[:, cols(k)], new_sem.at[k % 2, n])

    def grads(k):
        @pl.when(k >= 3)
        def _():
            for n in range(6):
                z_copy(k - 3, n).wait_send()

        s = k % 3

        @pl.when(k == 0)
        def _():
            rows_in(0, 2).wait()
            ha_load.wait()

        @pl.when(k == 6)
        def _():
            for q in range(4):
                rows_in(1, q).wait()

        g_send[s, 1] = product(k, 2).astype(bf)
        z_copy(k, 0).start()
        z_copy(k, 1).start()

        @pl.when(k == 0)
        def _():
            for q in (1, 3, 0):
                rows_in(0, q).wait()

        g_send[s, 0] = product(k, 1).astype(bf)
        z_copy(k, 2).start()
        g_send[s, 2] = product(k, 3).astype(bf)
        z_copy(k, 3).start()

    def relay(k):
        s = k % 3
        z_copy(k, 0).wait_recv()
        g_send[s, 0, lo] = (g_send[s, 0, lo].astype(f32) + r1[k, 0].astype(f32)).astype(bf)
        z_copy(k, 4).start()
        z_copy(k, 1).wait_recv()
        g_send[s, 2, hi] = (g_send[s, 2, hi].astype(f32) + r1[k, 1].astype(f32)).astype(bf)
        z_copy(k, 5).start()

    def gather_z(k):
        own = product(k, 0)
        for n in (2, 3, 4, 5):
            z_copy(k, n).wait_recv()
        raw_sum = own + r2[k, 0].astype(f32) + r2[k, 1].astype(f32)

        @pl.when(k >= 3)
        def _():
            h_copy(k - 3).wait_send()

        mine_first = h == 0
        x_send[k % 3] = jnp.where(mine_first, raw_sum[eighth:], raw_sum[:eighth]).astype(bf)
        h_copy(k).start()
        pick[k % 3] = jnp.where(mine_first, raw_sum[:eighth], raw_sum[eighth:])
        for n in range(2):
            state_in(k, n).start()

    def adam(k):
        h_copy(k).wait_recv()
        g = pick[k % 3] + x_recv[k].astype(f32)
        for n in range(2):
            state_in(k, n).wait()

        @pl.when(k >= 2)
        def _():
            for n in range(2):
                state_out(k - 2, n).wait()

        s = k % 2
        m1 = beta_one * m_stage[k % 3] + (1.0 - beta_one) * g
        v1 = beta_two * v_stage[k % 3] + (1.0 - beta_two) * g * g
        m_new[s] = m1
        v_new[s] = v1
        m_send[k] = m1.astype(bf)
        v_send[k] = v1.astype(bf)
        for n in range(2):
            m_copy(k, n).start()
            state_out(k, n).start()

    def wide(j):
        return pl.ds(pl.multiple_of(j * dw, dw), dw)

    def w_copy(j):
        rows = pl.ds(pl.multiple_of(j * dw, dw), dw)
        return pltpu.make_async_copy(w.at[rows, pl.ds(0, hid2)], w_stage.at[j % 2], load.at[10 + j % 2])

    def s_copy(j):
        return remote(s_send.at[j % 2], s_recv.at[j], ss_sem.at[j % 2], sr_sem.at[j], sib)

    def l_copy(j):
        return remote(l_send.at[j % 4], l_recv.at[j], ls_sem.at[j % 4], lr_sem.at[j], across)

    def y_copy(j, n):
        src = (l_own.at[j, 2, pl.ds(0, 64)], l_own.at[j, 2, pl.ds(64, 64)], y_send.at[j, 0], y_send.at[j, 1])[n]
        dst = (y1.at[j, 0], y1.at[j, 1], y2.at[j, 0], y2.at[j, 1])[n]
        return remote(src, dst, ys_sem.at[j, n], yr_sem.at[j, n], up_y if n % 2 == 0 else down_y)

    def t_copy(j):
        return pltpu.make_async_copy(t_out.at[j % 2], tok_grad.at[:, wide(j)], t_sem.at[j % 2])

    def inputs_back(j):
        w_copy(j).wait()

        @pl.when(j >= 2)
        def _():
            s_copy(j - 2).wait_send()

        b = j % 2
        dx = (
            lax.dot_general(
                ha[:, pl.ds(0, hid2)], w_stage[j % 2], (((1,), (1,)), ((), ())), preferred_element_type=f32
            )
            * scale_w
        ).astype(bf)
        for r in range(8):
            at = ORDER.index(r) * pair
            back = lax.dot_general(
                onehot[r], dx[at : at + pair], (((0,), (0,)), ((), ())), preferred_element_type=f32
            ).astype(bf)
            s_own[b, r] = back[:128]
            s_send[b, r] = back[128:]
        s_copy(j).start()

        @pl.when(j + 2 < n_col)
        def _():
            w_copy(j + 2).start()

    def add_core(j):
        b = j % 2
        s_copy(j).wait_recv()

        @pl.when(j >= 4)
        def _():
            l_copy(j - 4).wait_send()

        for dy in range(4):
            l_send[j % 4, dy] = (s_own[b, 2 * dy + 1].astype(f32) + s_recv[j, 2 * dy + 1].astype(f32)).astype(bf)
        l_copy(j).start()
        for dy in range(4):
            l_own[j, dy] = (s_own[b, 2 * dy].astype(f32) + s_recv[j, 2 * dy].astype(f32)).astype(bf)

    def add_across(j):
        l_copy(j).wait_recv()
        for dy in (2, 1, 3, 0):
            l_own[j, dy] = (l_own[j, dy].astype(f32) + l_recv[j, dy].astype(f32)).astype(bf)
        y_copy(j, 0).start()
        y_copy(j, 1).start()

    def add_relay(j):
        top, low = pl.ds(0, 64), pl.ds(64, 64)
        y_copy(j, 0).wait_recv()
        y_copy(j, 1).wait_recv()

        y_send[j, 0, top] = (l_own[j, 1, top].astype(f32) + y1[j, 0].astype(f32)).astype(bf)
        y_send[j, 0, low] = l_own[j, 1, low]
        y_send[j, 1, top] = l_own[j, 3, top]
        y_send[j, 1, low] = (l_own[j, 3, low].astype(f32) + y1[j, 1].astype(f32)).astype(bf)
        y_copy(j, 2).start()
        y_copy(j, 3).start()

    def add_last(j):
        @pl.when(j >= 2)
        def _():
            t_copy(j - 2).wait()

        b = j % 2

        y_copy(j, 2).wait_recv()
        y_copy(j, 3).wait_recv()
        t_out[b] = (l_own[j, 0].astype(f32) + y2[j, 0].astype(f32) + y2[j, 1].astype(f32)).astype(bf)
        t_copy(j).start()

    w_copy(0).start()
    w_copy(1).start()

    def twice(body):
        def both(i):
            body(2 * i)
            body(2 * i + 1)

        return both

    def stage(t, delay, count, body):
        k = t - delay

        @pl.when((k >= 0) & (k < count))
        def _():
            body(k)

    @pl.loop(0, n_chunk + 3)
    def _(t):
        stage(t, 0, n_chunk, grads)

        @pl.when(t == 0)
        def _():
            onehot_load.wait()
            far_w.start()

        stage(t, 1, n_col // 2, twice(add_core))
        stage(t, 0, n_col // 2, twice(inputs_back))
        stage(t, 0, n_chunk, relay)
        stage(t, 1, n_chunk, gather_z)
        stage(t, 2, n_chunk, adam)
        stage(t, 3, n_col // 2, twice(add_across))
        stage(t, 4, n_col // 2, twice(add_relay))
        stage(t, 6, n_col // 2, twice(add_last))

    for k in range(n_chunk - 3, n_chunk):
        for n in range(6):
            z_copy(k, n).wait_send()
    for k in range(n_chunk - 3, n_chunk):
        h_copy(k).wait_send()
    for k in range(n_chunk - 2, n_chunk):
        for n in range(2):
            state_out(k, n).wait()
    for j in range(n_col - 2, n_col):
        s_copy(j).wait_send()
        t_copy(j).wait()
    for j in range(n_col - 4, n_col):
        l_copy(j).wait_send()
    for j in range(n_col):
        for n in range(4):
            y_copy(j, n).wait_send()
    far_w.wait()
    for k in range(n_chunk):
        for n in range(2):
            m_copy(k, n).wait()


def reduce(xt, ha, onehot, weights, moment_one, moment_two, scales):
    width, total = weights.shape
    rows = moment_one.shape[0]
    bf, f32 = jnp.bfloat16, jnp.float32
    sems = pltpu.SemaphoreType.DMA
    small = jax.ShapeDtypeStruct((rows, total), bf)
    large = jax.ShapeDtypeStruct((rows, total), f32)
    return pl.pallas_call(
        functools.partial(reduce_kernel, scales),
        name="reduce",
        out_shape=(jax.ShapeDtypeStruct((128, width), bf), large, large, small, small, small),
        in_specs=[ANY] * 6,
        out_specs=(ANY,) * 6,
        scratch_shapes=[
            pltpu.VMEM((2, 4, 640, 1024), bf),
            pltpu.VMEM((1024, 2304), bf),
            pltpu.VMEM((8, 128, 256), bf),
            pltpu.VMEM((3, 3, 640, 256), bf),
            pltpu.VMEM((9, 2, 320, 256), bf),
            pltpu.VMEM((9, 2, 640, 256), bf),
            pltpu.VMEM((3, 320, 256), bf),
            pltpu.VMEM((9, 320, 256), bf),
            pltpu.VMEM((3, 320, 256), f32),
            pltpu.VMEM((3, 320, 256), f32),
            pltpu.VMEM((2, 320, 256), f32),
            pltpu.VMEM((2, 320, 256), f32),
            pltpu.VMEM((9, 320, 256), bf),
            pltpu.VMEM((9, 320, 256), bf),
            pltpu.VMEM((2, 256, 1536), bf),
            pltpu.VMEM((3, 320, 256), f32),
            pltpu.VMEM((2, 8, 128, 256), bf),
            pltpu.VMEM((2, 8, 128, 256), bf),
            pltpu.VMEM((10, 8, 128, 256), bf),
            pltpu.VMEM((10, 4, 128, 256), bf),
            pltpu.VMEM((10, 4, 128, 256), bf),
            pltpu.VMEM((4, 4, 128, 256), bf),
            pltpu.VMEM((10, 2, 64, 256), bf),
            pltpu.VMEM((10, 2, 128, 256), bf),
            pltpu.VMEM((10, 2, 128, 256), bf),
            pltpu.VMEM((2, 128, 256), bf),
            sems(()),
            sems(()),
            sems((12,)),
            sems((3, 6)),
            sems((9, 2)),
            sems((9, 4)),
            sems((3,)),
            sems((9,)),
            sems((3, 2)),
            sems((2, 2)),
            sems((9, 2)),
            sems((9, 2)),
            sems((2,)),
            sems((10,)),
            sems((4,)),
            sems((10,)),
            sems((10, 4)),
            sems((10, 4)),
            sems((2,)),
        ],
        compiler_params=pltpu.CompilerParams(
            collective_id=2, has_side_effects=True, vmem_limit_bytes=60 * 2**20
        ),
    )(xt, ha, onehot, weights, moment_one, moment_two)


def place_kernel(info, w, w_got, m_own, v_own, m_got, v_got, w_new, m_new, v_new):
    def write(rows, first, second):
        weight = rows.astype(jnp.float32)
        first_hat = first * (1.0 / (1.0 - beta_one**adam_step))
        second_hat = second * (1.0 / (1.0 - beta_two**adam_step))
        m_new[0] = first
        v_new[0] = second
        w_new[0] = (
            weight - learn_rate * (first_hat / (jnp.sqrt(second_hat) + adam_eps) + decay_rate * weight)
        ).astype(w_new.dtype)

    @pl.when(info[0] == 0)
    def _():
        write(w[...], m_own[...], v_own[...])

    @pl.when(info[0] != 0)
    def _():
        write(w_got[...], m_got[...].astype(jnp.float32), v_got[...].astype(jnp.float32))


def place(info, weights, w_got, m_own, v_own, m_got, v_got):
    rows, total = m_own.shape
    step = 160
    steps = rows // step
    stay = pl.BlockSpec((step, total), lambda i, f: (jnp.where(f[0] == 0, i, 0), 0))
    move = pl.BlockSpec((step, total), lambda i, f: (jnp.where(f[0] == 0, 0, i), 0))
    old = pl.BlockSpec((step, total), lambda i, f: (f[1] * steps + jnp.where(f[0] == 0, i, 0), 0))
    out = pl.BlockSpec((1, step, total), lambda i, f: (0, i, 0))
    return pl.pallas_call(
        place_kernel,
        name="place",
        grid_spec=pltpu.PrefetchScalarGridSpec(
            num_scalar_prefetch=1,
            grid=(steps,),
            in_specs=[old, move, stay, stay, move, move],
            out_specs=(out, out, out),
        ),
        out_shape=(
            jax.ShapeDtypeStruct((1, rows, total), jnp.bfloat16),
            jax.ShapeDtypeStruct((1, rows, total), jnp.float32),
            jax.ShapeDtypeStruct((1, rows, total), jnp.float32),
        ),
        compiler_params=pltpu.CompilerParams(vmem_limit_bytes=60 * 2**20),
    )(info, weights, w_got, m_own, v_own, m_got, v_got)


def shards(tokens, expert_ids, gate_q, cotangent, placement, weights, moment_one, moment_two):
    my_slot = lax.axis_index("expert")
    dp_index = lax.axis_index("dp")
    width = tokens.shape[1]
    hidden = weights.shape[2] // 3
    scales = (width ** (-0.5), hidden ** (-0.5))
    pack = jnp.concatenate(
        [
            jnp.pad(expert_ids.T, ((0, 2), (0, 0)), constant_values=-1),
            jnp.pad(gate_q.T, ((0, 2), (0, 0))),
        ],
        axis=0,
    )
    xt, ha, onehot, _ = dispatch(tokens, cotangent, pack, weights[0], scales)
    token_grad, m_own, v_own, w_got, m_got, v_got = reduce(
        xt, ha, onehot, weights[0], moment_one[0], moment_two[0], scales
    )
    moving = (placement[my_slot] != my_slot).astype(jnp.int32)
    info = jnp.stack([moving, dp_index.astype(jnp.int32)])
    new_w, new_m, new_v = place(info, weights[0], w_got, m_own, v_own, m_got, v_got)
    return (token_grad, new_w, new_m, new_v)


def solution(mesh):
    placed = (
        P(("dp", "expert"), None),
        P(("dp", "expert"), None),
        P(("dp", "expert"), None),
        P(("dp", "expert"), None),
        P(),
        P("expert", None, None),
        P("expert", "dp", None),
        P("expert", "dp", None),
    )
    return jax.shard_map(
        shards,
        mesh=mesh,
        in_specs=placed,
        out_specs=(
            P(("dp", "expert"), None),
            P("expert", "dp", None),
            P("expert", "dp", None),
            P("expert", "dp", None),
        ),
        check_vma=False,
    )
```

```python
import functools

import jax
import jax.numpy as jnp
from jax import lax
from jax.experimental import pallas as pl
from jax.experimental.pallas import tpu as pltpu
from jax.sharding import PartitionSpec as P

beta_one = 0.9
beta_two = 0.95
learn_rate = 0.02
decay_rate = 0.1
adam_eps = 1e-08
adam_step = 20.0

MESH = pl.DeviceIdType.MESH
ANY = pl.BlockSpec(memory_space=pl.ANY)
VMEM = pl.BlockSpec(memory_space=pltpu.VMEM)

ORDER = (0, 1, 2, 3, 6, 7, 4, 5)
BATCHES = ((0, 1), (2, 3, 6, 7), (4, 5))


def coords():
    dp = lax.axis_index("dp")
    e = lax.axis_index("expert")
    return dp, e, e // 4, (e // 2) % 2, e % 2


def peer(dy, dl, dc):
    dp, _, y, l, c = coords()
    y2 = (y + dy) % 4 if dy else y
    l2 = 1 - l if dl else l
    c2 = 1 - c if dc else c
    return (dp, y2 * 4 + l2 * 2 + c2)


def dispatch_kernel(
    scales,
    tok,
    cot,
    pack,
    w,
    xt_out,
    ha_out,
    p_out,
    gathered,
    ids,
    mrow,
    grow,
    gcol,
    onehot,
    wv,
    stage,
    xc,
    xt,
    pre,
    ha,
    psend,
    precv,
    send,
    recv,
    local,
    outs,
):
    scale_w, scale_h = scales
    _, me, _, _, _ = coords()
    cap, pair = 56, 128
    hid = pre.shape[1] // 2
    chips = [(dy, dl, 0) for dy in range(4) for dl in range(2)][1:]
    others = chips + [(0, 0, 1)]

    barrier = pltpu.get_barrier_semaphore()
    for o in others:
        pl.semaphore_signal(barrier, inc=1, device_id=peer(*o), device_id_type=MESH)
    pl.semaphore_wait(barrier, len(others))

    packs = []
    for n, (dy, dl, dc) in enumerate(chips):
        packs.append(
            pltpu.make_async_remote_copy(
                src_ref=pack,
                dst_ref=ids.at[0, ((4 - dy) % 4) * 2 + dl],
                send_sem=psend.at[n],
                recv_sem=precv.at[n],
                device_id=peer(dy, dl, dc),
                device_id_type=MESH,
            )
        )
    for d in packs:
        d.start()
    ids[0, 0] = pack[...]

    flight = {}

    def go(i, key, src, r, rows, to):
        n = len(flight)
        d = pltpu.make_async_remote_copy(
            src_ref=src,
            dst_ref=gathered.at[i, r, pl.ds(128 * to[2] + rows[0], rows[1] - rows[0])],
            send_sem=send.at[n],
            recv_sem=recv.at[n],
            device_id=peer(*to),
            device_id_type=MESH,
        )
        d.start()
        flight[(i, key)] = d

    UP, DOWN, ACROSS, SIB = (1, 0, 0), (3, 0, 0), (0, 1, 0), (0, 0, 1)
    own = (tok, cot)

    def mine(i, lo, hi):
        return own[i].at[pl.ds(lo, hi - lo)]

    def got(i, r, lo, hi):
        return gathered.at[i, r, pl.ds(lo, hi - lo)]

    def share(i, r, lo, hi):
        go(i, ("S", r, lo), got(i, r, lo, hi), r, (lo, hi), SIB)

    def land(i, key):
        flight[(i, key)].wait_recv()

    cut = (80, 64)
    fork = ((48, 32), (32, 32))
    fork_b = (96, 96)

    def first(i):
        a = cut[i]
        go(i, "A1", mine(i, 0, a), 1, (0, a), ACROSS)
        go(i, "B1p", mine(i, a, 128), 6, (a, 128), UP)
        go(i, "B1m", mine(i, a, 128), 2, (a, 128), DOWN)
        go(i, "A2p0", mine(i, 0, a), 6, (0, a), UP)
        go(i, "A2m0", mine(i, 0, a), 2, (0, a), DOWN)
        go(i, "B30", mine(i, a, 128), 1, (a, 128), ACROSS)
        go(i, ("S", 0, 0), own[i], 0, (0, 128), SIB)

    def second(i):
        a, f = cut[i], fork[i][0]
        land(i, "A1")
        go(i, "A2p1", got(i, 1, 0, a), 7, (0, a), UP)
        go(i, "A2m1", got(i, 1, 0, a), 3, (0, a), DOWN)
        share(i, 1, 0, a)
        land(i, "A2p0")
        go(i, "A3p0", got(i, 6, 0, f), 4, (0, f), UP)
        share(i, 6, 0, a)
        land(i, "A2m0")
        go(i, "A3m0", got(i, 2, f, a), 4, (f, a), DOWN)
        share(i, 2, 0, a)

    def third(i):
        a, b = cut[i], fork_b[i]
        land(i, "B1p")
        go(i, "B33", got(i, 6, a, 128), 7, (a, 128), ACROSS)
        go(i, "B2p", got(i, 6, a, b), 4, (a, b), UP)
        share(i, 6, a, 128)
        land(i, "B1m")
        go(i, "B31", got(i, 2, a, 128), 3, (a, 128), ACROSS)
        go(i, "B2m", got(i, 2, b, 128), 4, (b, 128), DOWN)
        share(i, 2, a, 128)
        land(i, "B30")
        share(i, 1, a, 128)

    def fourth(i):
        a, f = cut[i], fork[i][1]
        land(i, "A2p1")
        go(i, "A3p1", got(i, 7, 0, f), 5, (0, f), UP)
        share(i, 7, 0, a)
        land(i, "A2m1")
        go(i, "A3m1", got(i, 3, f, a), 5, (f, a), DOWN)
        share(i, 3, 0, a)
        land(i, "B2p")
        land(i, "B2m")
        go(i, "B32", got(i, 4, a, 128), 5, (a, 128), ACROSS)
        land(i, "A3p0")
        land(i, "A3m0")
        share(i, 4, 0, a)
        share(i, 4, a, 128)
        land(i, "B33")
        share(i, 7, a, 128)
        land(i, "B31")
        share(i, 3, a, 128)

    def fifth(i):
        a = cut[i]
        land(i, "A3p1")
        land(i, "A3m1")
        share(i, 5, 0, a)
        land(i, "B32")
        share(i, 5, a, 128)

    def fetch(i, batch):
        copies = []
        for n, r in enumerate(batch):
            if r == 0:
                land(i, ("S", 0, 0))
                copies.append(pltpu.make_async_copy(own[i], stage.at[n, pl.ds(0, 128)], local.at[n]))
                copies.append(
                    pltpu.make_async_copy(
                        gathered.at[i, 0, pl.ds(128, 128)], stage.at[n, pl.ds(128, 128)], local.at[4]
                    )
                )
            else:
                land(i, ("S", r, 0))
                land(i, ("S", r, cut[i]))
                copies.append(pltpu.make_async_copy(gathered.at[i, r], stage.at[n], local.at[n]))
        for d in copies:
            d.start()
        for d in copies:
            d.wait()

    def pick(i, batch):
        fetch(i, batch)
        for n, r in enumerate(batch):
            at = ORDER.index(r) * pair
            rows = jnp.dot(onehot[r], stage[n], preferred_element_type=jnp.float32)
            if i == 1:
                rows = rows * gcol[pl.ds(at, pair), :]
            rows = rows.astype(jnp.bfloat16)
            xc[pl.ds(n * pair, pair), :] = rows
            for col in range(0, rows.shape[1], 128):
                xt[i, pl.ds(col, 128), pl.ds(at, pair)] = rows[:, col : col + 128].T
        at, size = span(batch)
        out(xt.at[i, :, pl.ds(at, size)], xt_out.at[i, :, pl.ds(at, size)])

    def out(src, dst):
        d = pltpu.make_async_copy(src, dst, outs.at[len(written)])
        d.start()
        written.append(d)

    written = []

    def span(batch):
        return ORDER.index(batch[0]) * pair, len(batch) * pair

    def forward(batch):
        at, size = span(batch)
        wide = 512

        @pl.loop(0, 2 * hid // wide)
        def _(n):
            cols = pl.ds(pl.multiple_of(n * wide, wide), wide)
            pre[pl.ds(at, size), cols] = (
                jnp.dot(xc[pl.ds(0, size), :], wv[:, cols], preferred_element_type=jnp.float32)
                * scale_w
            )

    def backward(batch):
        at, size = span(batch)
        wide = 256

        @pl.loop(0, hid // wide)
        def _(n):
            def cols(start):
                return pl.ds(pl.multiple_of(start + n * wide, wide), wide)

            rows = pl.ds(at, size)
            da = (
                jnp.dot(xc[pl.ds(0, size), :], wv[:, cols(2 * hid)], preferred_element_type=jnp.float32)
                * scale_h
            )
            gate = pre[rows, cols(0)]
            up = pre[rows, cols(hid)]
            sig = jax.nn.sigmoid(gate)
            gs = gate * sig
            ha[rows, cols(0)] = (da * up * sig * (1.0 + gate * (1.0 - sig))).astype(jnp.bfloat16)
            ha[rows, cols(hid)] = (da * gs).astype(jnp.bfloat16)
            ha[rows, cols(2 * hid)] = (gs * up).astype(jnp.bfloat16)

        out(ha.at[pl.ds(at, size)], ha_out.at[pl.ds(at, size)])

    first(0)
    weights_in = pltpu.make_async_copy(w, wv, local.at[5])
    weights_in.start()
    for d in packs:
        d.wait_recv()
    swap = pltpu.make_async_remote_copy(
        src_ref=ids.at[0],
        dst_ref=ids.at[1],
        send_sem=psend.at[7],
        recv_sem=precv.at[7],
        device_id=peer(*SIB),
        device_id_type=MESH,
    )
    swap.start()
    second(0)
    swap.wait_recv()
    for r in range(8):
        for core in range(2):
            s = 2 * r + core
            chosen = ids[core, r, 0:8, :] == me
            mrow[s : s + 1, :] = jnp.sum(jnp.where(chosen, 1.0, 0.0), axis=0, keepdims=True)
            grow[s : s + 1, :] = jnp.sum(
                jnp.where(chosen, ids[core, r, 8:16, :].astype(jnp.float32), 0.0), axis=0, keepdims=True
            ) * (1.0 / 65536.0)
    before = (
        lax.broadcasted_iota(jnp.int32, (128, 128), 0) < lax.broadcasted_iota(jnp.int32, (128, 128), 1)
    ).astype(jnp.bfloat16)
    position = jnp.dot(mrow[...].astype(jnp.bfloat16), before, preferred_element_type=jnp.float32)
    mrow[...] = jnp.where(mrow[...] > 0.5, position, -1000.0)
    slot = lax.broadcasted_iota(jnp.int32, (pair, 256), 0).astype(jnp.float32)
    for r in range(8):
        place = jnp.concatenate([mrow[2 * r : 2 * r + 1, :], mrow[2 * r + 1 : 2 * r + 2, :] + cap], axis=1)
        gate_row = jnp.concatenate([grow[2 * r : 2 * r + 1, :], grow[2 * r + 1 : 2 * r + 2, :]], axis=1)
        hit = jnp.where(slot == place, 1.0, 0.0)
        onehot[r] = hit.astype(jnp.bfloat16)
        gcol[pl.ds(ORDER.index(r) * pair, pair), :] = jnp.sum(hit * gate_row, axis=1, keepdims=True)
    out(onehot, p_out)
    third(0)
    first(1)
    pick(0, BATCHES[0])
    weights_in.wait()
    forward(BATCHES[0])
    fourth(0)
    second(1)
    pick(0, BATCHES[1])
    forward(BATCHES[1])
    fifth(0)
    third(1)
    pick(0, BATCHES[2])
    forward(BATCHES[2])
    pick(1, BATCHES[0])
    backward(BATCHES[0])
    fourth(1)
    pick(1, BATCHES[1])
    backward(BATCHES[1])
    fifth(1)
    pick(1, BATCHES[2])
    backward(BATCHES[2])
    for d in packs:
        d.wait_send()
    swap.wait_send()
    for d in flight.values():
        d.wait_send()
    for d in written:
        d.wait()


def dispatch(tokens, cotangent, pack, weights, scales):
    width = tokens.shape[1]
    total = weights.shape[1]
    hid = total // 3
    slots = 1024
    bf, f32 = jnp.bfloat16, jnp.float32
    sems = pltpu.SemaphoreType.DMA
    return pl.pallas_call(
        functools.partial(dispatch_kernel, scales),
        name="dispatch",
        out_shape=(
            jax.ShapeDtypeStruct((2, width, slots), bf),
            jax.ShapeDtypeStruct((slots, total), bf),
            jax.ShapeDtypeStruct((8, 128, 256), bf),
            jax.ShapeDtypeStruct((2, 8, 256, width), bf),
        ),
        in_specs=[ANY, ANY, VMEM, ANY],
        out_specs=(ANY,) * 4,
        scratch_shapes=[
            pltpu.VMEM((2, 8, 16, 128), jnp.int32),
            pltpu.VMEM((16, 128), f32),
            pltpu.VMEM((16, 128), f32),
            pltpu.VMEM((slots, 1), f32),
            pltpu.VMEM((8, 128, 256), bf),
            pltpu.VMEM((width, total), bf),
            pltpu.VMEM((4, 256, width), bf),
            pltpu.VMEM((512, width), bf),
            pltpu.VMEM((2, width, slots), bf),
            pltpu.VMEM((slots, 2 * hid), f32),
            pltpu.VMEM((slots, total), bf),
            sems((8,)),
            sems((8,)),
            sems((64,)),
            sems((64,)),
            sems((6,)),
            sems((10,)),
        ],
        compiler_params=pltpu.CompilerParams(
            collective_id=1, has_side_effects=True, vmem_limit_bytes=60 * 2**20
        ),
    )(tokens, cotangent, pack, weights)


def reduce_kernel(
    scales,
    xt_in,
    ha_in,
    p_in,
    w,
    m_in,
    v_in,
    tok_grad,
    m_out,
    v_out,
    w_got,
    m_got,
    v_got,
    xt,
    ha,
    onehot,
    g_send,
    r1,
    r2,
    x_send,
    x_recv,
    m_stage,
    v_stage,
    m_new,
    v_new,
    m_send,
    v_send,
    w_stage,
    pick,
    s_send,
    s_own,
    s_recv,
    l_recv,
    l_own,
    l_send,
    y1,
    y2,
    y_send,
    t_out,
    far_send,
    far_recv,
    load,
    z_send,
    r1_sem,
    r2_sem,
    xs_sem,
    xr_sem,
    state,
    new_sem,
    ms_sem,
    mr_sem,
    ss_sem,
    sr_sem,
    ls_sem,
    lr_sem,
    ys_sem,
    yr_sem,
    t_sem,
):
    scale_w, scale_h = scales
    dp, e, y, l, c = coords()
    z, h = dp // 2, dp % 2
    bf, f32 = jnp.bfloat16, jnp.float32
    up_z = (((z + 1) % 4) * 2 + h, e)
    down_z = (((z + 3) % 4) * 2 + h, e)
    other_h = (z * 2 + 1 - h, e)
    far = peer(2, 0, 0)
    sib = peer(0, 0, 1)
    across = peer(0, 1, 0)
    up_y = peer(1, 0, 0)
    down_y = peer(3, 0, 0)

    n_chunk, n_col = 9, 10
    cw = 256
    dw = 256
    quarter, eighth = 640, 320
    hid2 = 1536
    pair = 128

    barrier = pltpu.get_barrier_semaphore()
    greet = [up_z, down_z, other_h, far, sib, across, up_y, down_y]
    for d in greet:
        pl.semaphore_signal(barrier, inc=1, device_id=d, device_id_type=MESH)

    def rows_in(i, q):
        start = pl.multiple_of(((z + q) % 4) * quarter, quarter)
        return pltpu.make_async_copy(xt_in.at[i, pl.ds(start, quarter)], xt.at[i, q], load.at[4 * i + q])

    rows_in(0, 2).start()
    ha_load = pltpu.make_async_copy(ha_in, ha, load.at[8])
    ha_load.start()
    for q in (1, 3, 0):
        rows_in(0, q).start()
    onehot_load = pltpu.make_async_copy(p_in, onehot, load.at[9])
    onehot_load.start()
    for q in (2, 1, 3, 0):
        rows_in(1, q).start()
    pl.semaphore_wait(barrier, len(greet))

    def remote(src, dst, ssem, rsem, to):
        return pltpu.make_async_remote_copy(
            src_ref=src, dst_ref=dst, send_sem=ssem, recv_sem=rsem, device_id=to, device_id_type=MESH
        )

    own_rows = pl.ds(pl.multiple_of(dp * eighth, eighth), eighth)
    far_w = remote(w.at[own_rows], w_got, far_send, far_recv, far)

    def cols(k):
        return pl.ds(pl.multiple_of(k * cw, cw), cw)

    def product(k, q):
        scale = jnp.where(k < 6, scale_w, scale_h).astype(f32)
        return (
            jnp.dot(xt[k // 6, q], ha[:, cols(k)], preferred_element_type=f32) * scale
        )

    lo, hi = pl.ds(0, eighth), pl.ds(eighth, eighth)

    def z_copy(k, n):
        s = k % 3
        src = (
            g_send.at[s, 1, lo],
            g_send.at[s, 1, hi],
            g_send.at[s, 0, hi],
            g_send.at[s, 2, lo],
            g_send.at[s, 0, lo],
            g_send.at[s, 2, hi],
        )[n]
        dst = (
            r1.at[k, 0],
            r1.at[k, 1],
            r2.at[k, 0, hi],
            r2.at[k, 1, lo],
            r2.at[k, 0, lo],
            r2.at[k, 1, hi],
        )[n]
        rsem = (r1_sem.at[k, 0], r1_sem.at[k, 1], r2_sem.at[k, 0], r2_sem.at[k, 1], r2_sem.at[k, 2], r2_sem.at[k, 3])[n]
        return remote(src, dst, z_send.at[s, n], rsem, up_z if n % 2 == 0 else down_z)

    def h_copy(k):
        return remote(x_send.at[k % 3], x_recv.at[k], xs_sem.at[k % 3], xr_sem.at[k], other_h)

    def m_copy(k, n):
        src = (m_send, v_send)[n].at[k]
        dst = (m_got, v_got)[n].at[k]
        return remote(src, dst, ms_sem.at[k, n], mr_sem.at[k, n], far)

    def state_in(k, n):
        return pltpu.make_async_copy((m_in, v_in)[n].at[:, cols(k)], (m_stage, v_stage)[n].at[k % 3], state.at[k % 3, n])

    def state_out(k, n):
        return pltpu.make_async_copy((m_new, v_new)[n].at[k % 2], (m_out, v_out)[n].at[:, cols(k)], new_sem.at[k % 2, n])

    def grads(k):
        @pl.when(k >= 3)
        def _():
            for n in range(6):
                z_copy(k - 3, n).wait_send()

        s = k % 3

        @pl.when(k == 0)
        def _():
            rows_in(0, 2).wait()
            ha_load.wait()

        @pl.when(k == 6)
        def _():
            for q in range(4):
                rows_in(1, q).wait()

        g_send[s, 1] = product(k, 2).astype(bf)
        z_copy(k, 0).start()
        z_copy(k, 1).start()

        @pl.when(k == 0)
        def _():
            for q in (1, 3, 0):
                rows_in(0, q).wait()

        g_send[s, 0] = product(k, 1).astype(bf)
        z_copy(k, 2).start()
        g_send[s, 2] = product(k, 3).astype(bf)
        z_copy(k, 3).start()

    def relay(k):
        s = k % 3
        z_copy(k, 0).wait_recv()
        g_send[s, 0, lo] = (g_send[s, 0, lo].astype(f32) + r1[k, 0].astype(f32)).astype(bf)
        z_copy(k, 4).start()
        z_copy(k, 1).wait_recv()
        g_send[s, 2, hi] = (g_send[s, 2, hi].astype(f32) + r1[k, 1].astype(f32)).astype(bf)
        z_copy(k, 5).start()

    def gather_z(k):
        own = product(k, 0)
        for n in (2, 3, 4, 5):
            z_copy(k, n).wait_recv()
        raw_sum = own + r2[k, 0].astype(f32) + r2[k, 1].astype(f32)

        @pl.when(k >= 3)
        def _():
            h_copy(k - 3).wait_send()

        mine_first = h == 0
        x_send[k % 3] = jnp.where(mine_first, raw_sum[eighth:], raw_sum[:eighth]).astype(bf)
        h_copy(k).start()
        pick[k % 3] = jnp.where(mine_first, raw_sum[:eighth], raw_sum[eighth:])
        for n in range(2):
            state_in(k, n).start()

    def adam(k):
        h_copy(k).wait_recv()
        g = pick[k % 3] + x_recv[k].astype(f32)
        for n in range(2):
            state_in(k, n).wait()

        @pl.when(k >= 2)
        def _():
            for n in range(2):
                state_out(k - 2, n).wait()

        s = k % 2
        m1 = beta_one * m_stage[k % 3] + (1.0 - beta_one) * g
        v1 = beta_two * v_stage[k % 3] + (1.0 - beta_two) * g * g
        m_new[s] = m1
        v_new[s] = v1
        m_send[k] = m1.astype(bf)
        v_send[k] = v1.astype(bf)
        for n in range(2):
            m_copy(k, n).start()
            state_out(k, n).start()

    def wide(j):
        return pl.ds(pl.multiple_of(j * dw, dw), dw)

    def w_copy(j):
        rows = pl.ds(pl.multiple_of(j * dw, dw), dw)
        return pltpu.make_async_copy(w.at[rows, pl.ds(0, hid2)], w_stage.at[j % 2], load.at[10 + j % 2])

    def s_copy(j):
        return remote(s_send.at[j % 2], s_recv.at[j], ss_sem.at[j % 2], sr_sem.at[j], sib)

    def l_copy(j):
        return remote(l_send.at[j % 4], l_recv.at[j], ls_sem.at[j % 4], lr_sem.at[j], across)

    def y_copy(j, n):
        src = (l_own.at[j, 2, pl.ds(0, 64)], l_own.at[j, 2, pl.ds(64, 64)], y_send.at[j, 0], y_send.at[j, 1])[n]
        dst = (y1.at[j, 0], y1.at[j, 1], y2.at[j, 0], y2.at[j, 1])[n]
        return remote(src, dst, ys_sem.at[j, n], yr_sem.at[j, n], up_y if n % 2 == 0 else down_y)

    def t_copy(j):
        return pltpu.make_async_copy(t_out.at[j % 2], tok_grad.at[:, wide(j)], t_sem.at[j % 2])

    def inputs_back(j):
        w_copy(j).wait()

        @pl.when(j >= 2)
        def _():
            s_copy(j - 2).wait_send()

        b = j % 2
        dx = (
            lax.dot_general(
                ha[:, pl.ds(0, hid2)], w_stage[j % 2], (((1,), (1,)), ((), ())), preferred_element_type=f32
            )
            * scale_w
        ).astype(bf)
        for r in range(8):
            at = ORDER.index(r) * pair
            back = lax.dot_general(
                onehot[r], dx[at : at + pair], (((0,), (0,)), ((), ())), preferred_element_type=f32
            ).astype(bf)
            s_own[b, r] = back[:128]
            s_send[b, r] = back[128:]
        s_copy(j).start()

        @pl.when(j + 2 < n_col)
        def _():
            w_copy(j + 2).start()

    def add_core(j):
        b = j % 2
        s_copy(j).wait_recv()

        @pl.when(j >= 4)
        def _():
            l_copy(j - 4).wait_send()

        for dy in range(4):
            l_send[j % 4, dy] = (s_own[b, 2 * dy + 1].astype(f32) + s_recv[j, 2 * dy + 1].astype(f32)).astype(bf)
        l_copy(j).start()
        for dy in range(4):
            l_own[j, dy] = (s_own[b, 2 * dy].astype(f32) + s_recv[j, 2 * dy].astype(f32)).astype(bf)

    def add_across(j):
        l_copy(j).wait_recv()
        for dy in (2, 1, 3, 0):
            l_own[j, dy] = (l_own[j, dy].astype(f32) + l_recv[j, dy].astype(f32)).astype(bf)
        y_copy(j, 0).start()
        y_copy(j, 1).start()

    def add_relay(j):
        top, low = pl.ds(0, 64), pl.ds(64, 64)
        y_copy(j, 0).wait_recv()
        y_copy(j, 1).wait_recv()

        y_send[j, 0, top] = (l_own[j, 1, top].astype(f32) + y1[j, 0].astype(f32)).astype(bf)
        y_send[j, 0, low] = l_own[j, 1, low]
        y_send[j, 1, top] = l_own[j, 3, top]
        y_send[j, 1, low] = (l_own[j, 3, low].astype(f32) + y1[j, 1].astype(f32)).astype(bf)
        y_copy(j, 2).start()
        y_copy(j, 3).start()

    def add_last(j):
        @pl.when(j >= 2)
        def _():
            t_copy(j - 2).wait()

        b = j % 2

        y_copy(j, 2).wait_recv()
        y_copy(j, 3).wait_recv()
        t_out[b] = (l_own[j, 0].astype(f32) + y2[j, 0].astype(f32) + y2[j, 1].astype(f32)).astype(bf)
        t_copy(j).start()

    w_copy(0).start()
    w_copy(1).start()

    def twice(body):
        def both(i):
            body(2 * i)
            body(2 * i + 1)

        return both

    def stage(t, delay, count, body):
        k = t - delay

        @pl.when((k >= 0) & (k < count))
        def _():
            body(k)

    @pl.loop(0, n_chunk + 3)
    def _(t):
        stage(t, 0, n_chunk, grads)

        @pl.when(t == 0)
        def _():
            onehot_load.wait()
            far_w.start()

        stage(t, 1, n_col // 2, twice(add_core))
        stage(t, 0, n_col // 2, twice(inputs_back))
        stage(t, 0, n_chunk, relay)
        stage(t, 2, n_col // 2, twice(add_across))
        stage(t, 3, n_col // 2, twice(add_relay))
        stage(t, 1, n_chunk, gather_z)
        stage(t, 2, n_chunk, adam)
        stage(t, 5, n_col // 2, twice(add_last))

    for k in range(n_chunk - 3, n_chunk):
        for n in range(6):
            z_copy(k, n).wait_send()
    for k in range(n_chunk - 3, n_chunk):
        h_copy(k).wait_send()
    for k in range(n_chunk - 2, n_chunk):
        for n in range(2):
            state_out(k, n).wait()
    for j in range(n_col - 2, n_col):
        s_copy(j).wait_send()
        t_copy(j).wait()
    for j in range(n_col - 4, n_col):
        l_copy(j).wait_send()
    for j in range(n_col):
        for n in range(4):
            y_copy(j, n).wait_send()
    far_w.wait()
    for k in range(n_chunk):
        for n in range(2):
            m_copy(k, n).wait()


def reduce(xt, ha, onehot, weights, moment_one, moment_two, scales):
    width, total = weights.shape
    rows = moment_one.shape[0]
    bf, f32 = jnp.bfloat16, jnp.float32
    sems = pltpu.SemaphoreType.DMA
    small = jax.ShapeDtypeStruct((rows, total), bf)
    large = jax.ShapeDtypeStruct((rows, total), f32)
    chunked = jax.ShapeDtypeStruct((total // 256, rows, 256), bf)
    return pl.pallas_call(
        functools.partial(reduce_kernel, scales),
        name="reduce",
        out_shape=(jax.ShapeDtypeStruct((128, width), bf), large, large, small, chunked, chunked),
        in_specs=[ANY] * 6,
        out_specs=(ANY,) * 6,
        scratch_shapes=[
            pltpu.VMEM((2, 4, 640, 1024), bf),
            pltpu.VMEM((1024, 2304), bf),
            pltpu.VMEM((8, 128, 256), bf),
            pltpu.VMEM((3, 3, 640, 256), bf),
            pltpu.VMEM((9, 2, 320, 256), bf),
            pltpu.VMEM((9, 2, 640, 256), bf),
            pltpu.VMEM((3, 320, 256), bf),
            pltpu.VMEM((9, 320, 256), bf),
            pltpu.VMEM((3, 320, 256), f32),
            pltpu.VMEM((3, 320, 256), f32),
            pltpu.VMEM((2, 320, 256), f32),
            pltpu.VMEM((2, 320, 256), f32),
            pltpu.VMEM((9, 320, 256), bf),
            pltpu.VMEM((9, 320, 256), bf),
            pltpu.VMEM((2, 256, 1536), bf),
            pltpu.VMEM((3, 320, 256), f32),
            pltpu.VMEM((2, 8, 128, 256), bf),
            pltpu.VMEM((2, 8, 128, 256), bf),
            pltpu.VMEM((10, 8, 128, 256), bf),
            pltpu.VMEM((10, 4, 128, 256), bf),
            pltpu.VMEM((10, 4, 128, 256), bf),
            pltpu.VMEM((4, 4, 128, 256), bf),
            pltpu.VMEM((10, 2, 64, 256), bf),
            pltpu.VMEM((10, 2, 128, 256), bf),
            pltpu.VMEM((10, 2, 128, 256), bf),
            pltpu.VMEM((2, 128, 256), bf),
            sems(()),
            sems(()),
            sems((12,)),
            sems((3, 6)),
            sems((9, 2)),
            sems((9, 4)),
            sems((3,)),
            sems((9,)),
            sems((3, 2)),
            sems((2, 2)),
            sems((9, 2)),
            sems((9, 2)),
            sems((2,)),
            sems((10,)),
            sems((4,)),
            sems((10,)),
            sems((10, 4)),
            sems((10, 4)),
            sems((2,)),
        ],
        compiler_params=pltpu.CompilerParams(
            collective_id=2, has_side_effects=True, vmem_limit_bytes=60 * 2**20
        ),
    )(xt, ha, onehot, weights, moment_one, moment_two)


def place_kernel(info, w, w_got, m_own, v_own, m_got, v_got, w_new, m_new, v_new):
    def write(cols, rows, first, second):
        weight = rows.astype(jnp.float32)
        first_hat = first * (1.0 / (1.0 - beta_one**adam_step))
        second_hat = second * (1.0 / (1.0 - beta_two**adam_step))
        m_new[0, :, cols] = first
        v_new[0, :, cols] = second
        w_new[0, :, cols] = (
            weight - learn_rate * (first_hat / (jnp.sqrt(second_hat) + adam_eps) + decay_rate * weight)
        ).astype(w_new.dtype)

    chunks, _, cw = m_got.shape
    stays = info[lax.axis_index("expert")] == lax.axis_index("expert")

    @pl.when(stays)
    def _():
        for k in range(chunks):
            cols = slice(k * cw, (k + 1) * cw)
            write(cols, w[:, cols], m_own[:, cols], v_own[:, cols])

    @pl.when(jnp.logical_not(stays))
    def _():
        for k in range(chunks):
            cols = slice(k * cw, (k + 1) * cw)
            write(cols, w_got[:, cols], m_got[k].astype(jnp.float32), v_got[k].astype(jnp.float32))


def place(info, weights, w_got, m_own, v_own, m_got, v_got):
    rows, total = m_own.shape
    step = 160
    steps = rows // step

    def here(i, f):
        return jnp.where(f[lax.axis_index("expert")] == lax.axis_index("expert"), i, 0)

    def there(i, f):
        return i - here(i, f)

    stay = pl.BlockSpec((step, total), lambda i, f: (here(i, f), 0))
    move = pl.BlockSpec((step, total), lambda i, f: (there(i, f), 0))
    parts = pl.BlockSpec((m_got.shape[0], step, m_got.shape[2]), lambda i, f: (0, there(i, f), 0))
    old = pl.BlockSpec((step, total), lambda i, f: (lax.axis_index("dp") * steps + here(i, f), 0))
    out = pl.BlockSpec((1, step, total), lambda i, f: (0, i, 0))
    return pl.pallas_call(
        place_kernel,
        name="place",
        grid_spec=pltpu.PrefetchScalarGridSpec(
            num_scalar_prefetch=1,
            grid=(steps,),
            in_specs=[old, move, stay, stay, parts, parts],
            out_specs=(out, out, out),
        ),
        out_shape=(
            jax.ShapeDtypeStruct((1, rows, total), jnp.bfloat16),
            jax.ShapeDtypeStruct((1, rows, total), jnp.float32),
            jax.ShapeDtypeStruct((1, rows, total), jnp.float32),
        ),
        compiler_params=pltpu.CompilerParams(vmem_limit_bytes=60 * 2**20),
    )(info, weights, w_got, m_own, v_own, m_got, v_got)


def shards(tokens, expert_ids, gate_q, cotangent, placement, weights, moment_one, moment_two):
    width = tokens.shape[1]
    hidden = weights.shape[2] // 3
    scales = (width ** (-0.5), hidden ** (-0.5))
    pack = jnp.concatenate(
        [
            jnp.pad(expert_ids.T, ((0, 2), (0, 0)), constant_values=-1),
            jnp.pad(gate_q.T, ((0, 2), (0, 0))),
        ],
        axis=0,
    )
    xt, ha, onehot, _ = dispatch(tokens, cotangent, pack, weights[0], scales)
    token_grad, m_own, v_own, w_got, m_got, v_got = reduce(
        xt, ha, onehot, weights[0], moment_one[0], moment_two[0], scales
    )
    new_w, new_m, new_v = place(placement, weights[0], w_got, m_own, v_own, m_got, v_got)
    return (token_grad, new_w, new_m, new_v)


def solution(mesh):
    placed = (
        P(("dp", "expert"), None),
        P(("dp", "expert"), None),
        P(("dp", "expert"), None),
        P(("dp", "expert"), None),
        P(),
        P("expert", None, None),
        P("expert", "dp", None),
        P("expert", "dp", None),
    )
    return jax.shard_map(
        shards,
        mesh=mesh,
        in_specs=placed,
        out_specs=(
            P(("dp", "expert"), None),
            P("expert", "dp", None),
            P("expert", "dp", None),
            P("expert", "dp", None),
        ),
        check_vma=False,
    )
```
